128 devices in a mesh: pipe: 8 (over x, y_lo), tensor: 4 (over z), dp: 4 (over y_hi, core).
Axes of the slice: x: 4, y: 4 (y_hi: 2, y_lo: 2; y = y_hi * 2 + y_lo), z: 4, core: 2. Of those that a mesh axis runs over, the one named last changes fastest.
Arguments:
- new_coeffs: bfloat16 [1024, 256], P('dp'), may hold values from -6 to 6
- loss_grad: bfloat16 [1024, 256], P('dp'), may hold values from -6 to 6
- sent_forward: bfloat16 [8, 1024, 256], P('pipe', 'dp'), may hold values from -6 to 6
- sent_backward: bfloat16 [8, 1024, 256], P('pipe', 'dp'), may hold values from -6 to 6
- stashed: bfloat16 [8, 1024, 256], P('pipe', 'dp'), may hold values from -6 to 6
- subspace: bfloat16 [4096, 256], replicated, may hold values from -0.09375 to 0.09375
- norm_gain: float32 [8, 4096], P('pipe'), may hold values from 0.5 to 1.5
- w_query: bfloat16 [8, 4096, 4096], P('pipe', None, 'tensor'), may hold values from -3 to 3
- w_key: bfloat16 [8, 4096, 512], P('pipe', None, 'tensor'), may hold values from -3 to 3
- w_value: bfloat16 [8, 4096, 512], P('pipe', None, 'tensor'), may hold values from -0.09375 to 0.09375
- w_output: bfloat16 [8, 4096, 4096], P('pipe', 'tensor'), may hold values from -0.09375 to 0.09375
Outputs:
- forward_out: bfloat16 [8, 1024, 256], P('pipe', 'dp')
- backward_out: bfloat16 [8, 1024, 256], P('pipe', 'dp')
- grad_query: bfloat16 [8, 4096, 4096], P('pipe', 'dp', 'tensor')
- grad_key: bfloat16 [8, 4096, 512], P('pipe', 'dp', 'tensor')
- grad_value: bfloat16 [8, 4096, 512], P('pipe', 'dp', 'tensor')
- grad_output: bfloat16 [8, 4096, 4096], P('pipe', 'tensor', 'dp')
- grad_gain: float32 [8, 4096], P('pipe')
The draws below stay inside these ranges and needn't reach their ends.
All inputs are finite; a program needn't handle non-finite values.
Results may differ from the reference program's by a relative error of at most 0.015.
Values may be sent and summed in bfloat16 or wider, within the bound.
A program may use at most 192 MiB of HBM per device.

```python
import math
import jax
import jax.numpy as jnp
from jax import lax

D = 4096
QH = 32
KVH = 4
HD = 128
R = 256
SEQ = 256
SECTIONS = 8
TOKENS = 1024
N_DP = 4


def shared_keys(key):
    base_keys = jax.random.normal(key, (SECTIONS, D, KVH * HD), jnp.float32)
    return jnp.clip(base_keys, -6.0, 6.0) / math.sqrt(D)


def draw_w_key(key, part):
    base_keys = shared_keys(key)
    return jnp.clip(base_keys, -3.0, 3.0).astype(jnp.bfloat16)


def draw_w_query(key, part):
    key = jax.random.fold_in(key, 5)
    own_part = jnp.clip(jax.random.normal(key, (SECTIONS, D, QH * HD), jnp.float32), -6.0, 6.0) / math.sqrt(D)
    return jnp.clip(own_part, -3.0, 3.0).astype(jnp.bfloat16)


def block_levels(stream_key, extent, pieces, low, top_value):
    loudness, own = 1.0, jax.random.fold_in(stream_key, 6)
    for axis_at, shards_of in pieces:
        draws = jnp.exp(jax.random.uniform(jax.random.fold_in(own, axis_at), (shards_of,), jnp.float32, low / len(pieces), top_value / len(pieces)))
        loudness = loudness * jnp.repeat(draws, extent[axis_at] // shards_of).reshape([-1 if axis == axis_at else 1 for axis in range(len(extent))])
    return loudness


def bell_draw(key, shape, spread, bound, pieces=(), held_as=jnp.bfloat16):
    entries = spread * jax.random.normal(key, shape, jnp.float32)
    if pieces:
        entries = entries * block_levels(key, shape, pieces, -0.22, 0.18)
    return jnp.clip(entries, -bound, bound).astype(held_as)


def setup_inputs(seed: int = 0) -> dict:
    key_of = jax.random.split(jax.random.key(seed), 12)
    return {
        "new_coeffs": bell_draw(key_of[0], (TOKENS, R), 1.0, 6.0, ((0, 4),)),
        "loss_grad": bell_draw(key_of[1], (TOKENS, R), 1.0, 6.0, ((0, 4),)),
        "sent_forward": bell_draw(key_of[2], (SECTIONS, TOKENS, R), 1.0, 6.0, ((0, 8), (1, 4))),
        "sent_backward": bell_draw(key_of[3], (SECTIONS, TOKENS, R), 1.0, 6.0, ((0, 8), (1, 4))),
        "stashed": bell_draw(key_of[4], (SECTIONS, TOKENS, R), 1.0, 6.0, ((0, 8), (1, 4))),
        "subspace": bell_draw(key_of[5], (D, R), D ** -0.5, 0.09375),
        "norm_gain": jnp.clip(1.0 + 0.1 * jax.random.normal(key_of[6], (SECTIONS, D), jnp.float32), 0.5, 1.5),
        "w_query": draw_w_query(jax.random.fold_in(key_of[11], 71), 0),
        "w_key": draw_w_key(jax.random.fold_in(key_of[11], 71), 0),
        "w_value": bell_draw(key_of[9], (SECTIONS, D, KVH * HD), D ** -0.5, 0.09375, ((0, 8), (2, 4))),
        "w_output": bell_draw(key_of[10], (SECTIONS, QH * HD, D), (QH * HD) ** -0.5, 0.09375, ((0, 8), (1, 4))),
    }


EPSILON = 1e-05
ROPE_BASE = 500000.0

def rope_tables(length, head_width):
    half_width = head_width // 2
    frequency = ROPE_BASE ** (-2.0 * jnp.arange(half_width, dtype=jnp.float32) / head_width)
    angles = jnp.arange(length, dtype=jnp.float32)[:, None] * frequency[None, :]
    angles = jnp.concatenate([angles, angles], axis=1)
    return (jnp.cos(angles), jnp.sin(angles))

def rotate_half(values):
    half_width = values.shape[-1] // 2
    return jnp.concatenate([-values[..., half_width:], values[..., :half_width]], axis=-1)

def apply_rope(values, cosine, sine_table):
    return values * cosine[:, None, :] + rotate_half(values) * sine_table[:, None, :]

def undo_rope(values, cosine, sine_table):
    return values * cosine[:, None, :] - rotate_half(values) * sine_table[:, None, :]

def forward_cache(coeffs, basis_wide, gain_row, query_w, key_w, value_w, cosine, sine_table):
    seq_count = coeffs.shape[0]
    length = coeffs.shape[1]
    decoded = jnp.einsum('ntr,dr->ntd', coeffs.astype(jnp.float32), basis_wide)
    root_mean = jnp.sqrt(lax.optimization_barrier(jnp.mean(decoded * decoded, axis=-1, keepdims=True)) + EPSILON)
    unit_rows = decoded / root_mean
    normed = (unit_rows * gain_row).astype(jnp.bfloat16)
    normed_wide = normed.astype(jnp.float32)
    query_rows = jnp.einsum('ntd,de->nte', normed_wide, query_w.astype(jnp.float32)).reshape(seq_count, length, QH, HD)
    query_rows = apply_rope(query_rows, cosine, sine_table).astype(jnp.bfloat16)
    key_rows = jnp.einsum('ntd,de->nte', normed_wide, key_w.astype(jnp.float32)).reshape(seq_count, length, KVH, HD)
    key_rows = apply_rope(key_rows, cosine, sine_table).astype(jnp.bfloat16)
    value_rows = jnp.einsum('ntd,de->nte', normed_wide, value_w.astype(jnp.float32)).reshape(seq_count, length, KVH, HD).astype(jnp.bfloat16)
    grouped = query_rows.reshape(seq_count, length, KVH, QH // KVH, HD)
    scores = jnp.einsum('ntkgd,nukd->nkgtu', grouped.astype(jnp.float32), key_rows.astype(jnp.float32)) / math.sqrt(HD)
    causal = jnp.arange(length)[:, None] >= jnp.arange(length)[None, :]
    scores = jnp.where(causal, scores, -jnp.inf)
    row_max = lax.optimization_barrier(jnp.max(scores, axis=-1, keepdims=True))
    exps = jnp.exp(scores - row_max)
    probs_full = exps / lax.optimization_barrier(jnp.sum(exps, axis=-1, keepdims=True))
    probs_low = probs_full.astype(jnp.bfloat16)
    mixed_heads = jnp.einsum('nkgtu,nukd->ntkgd', probs_low.astype(jnp.float32), value_rows.astype(jnp.float32))
    head_out = mixed_heads.astype(jnp.bfloat16).reshape(seq_count, length, QH * HD)
    return (decoded, root_mean, unit_rows, normed, grouped, key_rows, value_rows, probs_full, probs_low, head_out)

def reduce_parts(per_seq):
    rounded = lax.optimization_barrier(per_seq.astype(jnp.bfloat16))
    return lax.optimization_barrier(jnp.sum(rounded.astype(jnp.float32), axis=0)).astype(jnp.bfloat16)

def backward_section(coeffs, upstream, basis_wide, gain_row, query_w, key_w, value_w, output_w, cosine, sine_table):
    decoded, root_mean, unit_rows, normed, grouped, key_rows, value_rows, probs_full, probs_low, head_out = forward_cache(coeffs, basis_wide, gain_row, query_w, key_w, value_w, cosine, sine_table)
    seq_count = coeffs.shape[0]
    length = coeffs.shape[1]
    up_wide = jnp.einsum('ntr,dr->ntd', upstream.astype(jnp.float32), basis_wide)
    up_low = up_wide.astype(jnp.bfloat16)
    output_parts = jnp.einsum('nte,ntd->ned', head_out.astype(jnp.float32), up_low.astype(jnp.float32))
    grad_heads = jnp.einsum('ntd,ed->nte', up_low.astype(jnp.float32), output_w.astype(jnp.float32))
    grad_heads = grad_heads.astype(jnp.bfloat16).reshape(seq_count, length, KVH, QH // KVH, HD)
    grad_values = jnp.einsum('nkgtu,ntkgd->nukd', probs_low.astype(jnp.float32), grad_heads.astype(jnp.float32))
    grad_probs = jnp.einsum('ntkgd,nukd->nkgtu', grad_heads.astype(jnp.float32), value_rows.astype(jnp.float32))
    grad_scores = probs_full * (grad_probs - lax.optimization_barrier(jnp.sum(probs_full * grad_probs, axis=-1, keepdims=True))) / math.sqrt(HD)
    scores_low = grad_scores.astype(jnp.bfloat16).astype(jnp.float32)
    grad_query = jnp.einsum('nkgtu,nukd->ntkgd', scores_low, key_rows.astype(jnp.float32)).reshape(seq_count, length, QH, HD)
    grad_keys = jnp.einsum('nkgtu,ntkgd->nukd', scores_low, grouped.astype(jnp.float32))
    grad_query = undo_rope(grad_query, cosine, sine_table).astype(jnp.bfloat16).reshape(seq_count, length, QH * HD)
    grad_keys = undo_rope(grad_keys, cosine, sine_table).astype(jnp.bfloat16).reshape(seq_count, length, KVH * HD)
    grad_values = grad_values.astype(jnp.bfloat16).reshape(seq_count, length, KVH * HD)
    normed_wide = normed.astype(jnp.float32)
    query_parts = jnp.einsum('ntd,nte->nde', normed_wide, grad_query.astype(jnp.float32))
    key_parts = jnp.einsum('ntd,nte->nde', normed_wide, grad_keys.astype(jnp.float32))
    value_parts = jnp.einsum('ntd,nte->nde', normed_wide, grad_values.astype(jnp.float32))
    grad_normed = jnp.einsum('nte,de->ntd', grad_query.astype(jnp.float32), query_w.astype(jnp.float32))
    grad_normed = grad_normed + jnp.einsum('nte,de->ntd', grad_keys.astype(jnp.float32), key_w.astype(jnp.float32))
    grad_normed = grad_normed + jnp.einsum('nte,de->ntd', grad_values.astype(jnp.float32), value_w.astype(jnp.float32))
    grad_gain = lax.optimization_barrier(jnp.sum(grad_normed * unit_rows, axis=(0, 1)))
    scaled = grad_normed * gain_row
    middle = lax.optimization_barrier(jnp.mean(scaled * unit_rows, axis=-1, keepdims=True))
    grad_decoded = (scaled - unit_rows * middle) / root_mean
    back_coeffs = jnp.einsum('ntd,dr->ntr', up_wide + grad_decoded, basis_wide, precision=lax.Precision.HIGHEST).astype(jnp.bfloat16)
    return (back_coeffs, reduce_parts(query_parts), reduce_parts(key_parts), reduce_parts(value_parts), reduce_parts(output_parts), grad_gain)

def reference(new_coeffs, loss_grad, sent_forward, sent_backward, stashed, subspace, norm_gain, w_query, w_key, w_value, w_output):
    cosine, sine_table = rope_tables(SEQ, HD)
    basis_wide = subspace.astype(jnp.float32)
    forward_list = []
    backward_list = []
    query_list = []
    key_list = []
    value_list = []
    output_list = []
    gain_list = []
    for section_index in range(SECTIONS):
        if section_index == 0:
            inputs = new_coeffs
        else:
            inputs = sent_forward[section_index - 1]
        if section_index == SECTIONS - 1:
            upstream = loss_grad
        else:
            upstream = sent_backward[section_index + 1]
        inputs = inputs.reshape(N_DP, SEQ, R)
        upstream = upstream.reshape(N_DP, SEQ, R)
        gain_row = norm_gain[section_index]
        cache = forward_cache(inputs, basis_wide, gain_row, w_query[section_index], w_key[section_index], w_value[section_index], cosine, sine_table)
        attention = jnp.einsum('nte,ed->ntd', cache[9].astype(jnp.float32), w_output[section_index].astype(jnp.float32))
        forward_coeffs = jnp.einsum('ntd,dr->ntr', cache[0] + attention, basis_wide, precision=lax.Precision.HIGHEST).astype(jnp.bfloat16)
        forward_list.append(forward_coeffs.reshape(TOKENS, R))
        result = backward_section(stashed[section_index].reshape(N_DP, SEQ, R), upstream, basis_wide, gain_row, w_query[section_index], w_key[section_index], w_value[section_index], w_output[section_index], cosine, sine_table)
        backward_list.append(result[0].reshape(TOKENS, R))
        query_list.append(result[1])
        key_list.append(result[2])
        value_list.append(result[3])
        output_list.append(result[4])
        gain_list.append(result[5])
    return (jnp.stack(forward_list), jnp.stack(backward_list), jnp.stack(query_list), jnp.stack(key_list), jnp.stack(value_list), jnp.stack(output_list), jnp.stack(gain_list))
```

```python
import math

import jax
import jax.numpy as jnp
from jax import lax
from jax.sharding import PartitionSpec as P

HD = 128
EPSILON = 1e-05
ROPE_BASE = 500000.0
BF16 = jnp.bfloat16
F32 = jnp.float32


def shifted(x, axis, by):
    devices = lax.axis_size(axis)
    pairs = [(i, i + by) for i in range(devices) if 0 <= i + by < devices]
    return lax.ppermute(x, axis, pairs)


def rope_tables(length, head_width):
    half_width = head_width // 2
    frequency = ROPE_BASE ** (-2.0 * jnp.arange(half_width, dtype=F32) / head_width)
    angles = jnp.arange(length, dtype=F32)[:, None] * frequency[None, :]
    angles = jnp.concatenate([angles, angles], axis=1)
    return (jnp.cos(angles), jnp.sin(angles))


def rotate_half(values):
    half_width = values.shape[-1] // 2
    return jnp.concatenate([-values[..., half_width:], values[..., :half_width]], axis=-1)


def apply_rope(values, cosine, sine_table):
    return values * cosine[:, None, :] + rotate_half(values) * sine_table[:, None, :]


def undo_rope(values, cosine, sine_table):
    return values * cosine[:, None, :] - rotate_half(values) * sine_table[:, None, :]


def dot(spec, a, b):
    return jnp.einsum(spec, a, b, preferred_element_type=F32)


def heads(coeffs, gram, width, query_c, key_c, value_c, cosine, sine_table):
    length = coeffs.shape[0]
    wide = coeffs.astype(F32)
    projected = jnp.dot(wide, gram, precision=lax.Precision.HIGHEST)
    square = jnp.maximum(jnp.sum(projected * wide, axis=-1, keepdims=True), 0.0) / width
    inverse = 1.0 / jnp.sqrt(square + EPSILON)
    query_rows = (dot("tr,re->te", coeffs, query_c) * inverse).reshape(length, -1, HD)
    query_rows = apply_rope(query_rows, cosine, sine_table).astype(BF16)
    key_rows = (dot("tr,re->te", coeffs, key_c) * inverse).reshape(length, -1, HD)
    key_rows = apply_rope(key_rows, cosine, sine_table).astype(BF16)
    value_rows = (dot("tr,re->te", coeffs, value_c) * inverse).astype(BF16).reshape(length, -1, HD)
    key_heads = key_rows.shape[1]
    grouped = query_rows.reshape(length, key_heads, -1, HD)
    scores = dot("tkgd,ukd->kgtu", grouped, key_rows) / math.sqrt(HD)
    causal = jnp.arange(length)[:, None] >= jnp.arange(length)[None, :]
    scores = jnp.where(causal, scores, -jnp.inf)
    row_max = jnp.max(scores, axis=-1, keepdims=True)
    exps = jnp.exp(scores - row_max)
    probs_full = exps / jnp.sum(exps, axis=-1, keepdims=True)
    probs_low = probs_full.astype(BF16)
    head_out = dot("kgtu,ukd->tkgd", probs_low, value_rows).astype(BF16).reshape(length, -1)
    return projected, inverse, grouped, key_rows, value_rows, probs_full, probs_low, head_out


def body(
    new_coeffs,
    loss_grad,
    sent_forward,
    sent_backward,
    stashed,
    subspace,
    norm_gain,
    w_query,
    w_key,
    w_value,
    w_output,
):
    section_index = lax.axis_index("pipe")
    last_section = lax.axis_size("pipe") - 1
    arrived = shifted(sent_forward[0], "pipe", 1)
    returned = shifted(sent_backward[0], "pipe", -1)
    inputs = jnp.where(section_index == 0, new_coeffs, arrived)
    upstream = jnp.where(section_index == last_section, loss_grad, returned)
    saved = stashed[0]
    length = inputs.shape[0]
    width = subspace.shape[0]
    cosine, sine_table = rope_tables(length, HD)
    gain_row = norm_gain[0]
    query_w = w_query[0]
    key_w = w_key[0]
    value_w = w_value[0]
    output_w = w_output[0]
    basis_scaled = (subspace * gain_row[:, None]).astype(BF16)
    gram = dot("dr,ds->rs", subspace, subspace)
    query_c = dot("dr,de->re", basis_scaled, query_w).astype(BF16)
    key_c = dot("dr,de->re", basis_scaled, key_w).astype(BF16)
    value_c = dot("dr,de->re", basis_scaled, value_w).astype(BF16)
    output_c = dot("ed,dr->er", output_w, subspace).astype(BF16)
    tables = (gram, width, query_c, key_c, value_c, cosine, sine_table)
    projected, _, _, _, _, _, _, head_out = heads(inputs, *tables)
    forward_part = dot("te,er->tr", head_out, output_c)
    projected_b, inverse, grouped, key_rows, value_rows, probs_full, probs_low, head_out = heads(
        saved, *tables
    )
    key_heads = key_rows.shape[1]
    group_size = grouped.shape[2]
    output_term = dot("te,tr->er", head_out, upstream)
    grad_heads = dot("tr,er->te", upstream, output_c)
    grad_heads = grad_heads.astype(BF16).reshape(length, key_heads, group_size, HD)
    grad_values = dot("kgtu,tkgd->ukd", probs_low, grad_heads)
    grad_probs = dot("tkgd,ukd->kgtu", grad_heads, value_rows)
    centred = grad_probs - jnp.sum(probs_full * grad_probs, axis=-1, keepdims=True)
    scores_low = (probs_full * centred / math.sqrt(HD)).astype(BF16)
    grad_query = dot("kgtu,ukd->tkgd", scores_low, key_rows).reshape(length, -1, HD)
    grad_keys = dot("kgtu,tkgd->ukd", scores_low, grouped)
    grad_query = undo_rope(grad_query, cosine, sine_table).astype(BF16).reshape(length, -1)
    grad_keys = undo_rope(grad_keys, cosine, sine_table).astype(BF16).reshape(length, -1)
    grad_values = grad_values.astype(BF16).reshape(length, -1)
    scaled_coeffs = (saved * inverse).astype(BF16)
    query_term = dot("tr,te->re", scaled_coeffs, grad_query)
    key_term = dot("tr,te->re", scaled_coeffs, grad_keys)
    value_term = dot("tr,te->re", scaled_coeffs, grad_values)
    backward_part = dot("te,re->tr", grad_query, query_c)
    backward_part = backward_part + dot("te,re->tr", grad_keys, key_c)
    backward_part = backward_part + dot("te,re->tr", grad_values, value_c)
    forward_sum, backward_sum = lax.psum(
        (forward_part.astype(BF16), backward_part.astype(BF16)), "tensor"
    )
    forward_coeffs = (projected + forward_sum.astype(F32)).astype(BF16)
    backward_sum = backward_sum.astype(F32)
    middle = jnp.sum(backward_sum * saved, axis=-1, keepdims=True) * (inverse / width)
    grad_coeffs = (backward_sum - projected_b * (inverse * middle)) * inverse
    lifted = jnp.dot(upstream.astype(F32), gram, precision=lax.Precision.HIGHEST)
    backward_coeffs = (lifted + grad_coeffs).astype(BF16)
    query_term, key_term, value_term, output_term = lax.psum(
        (
            query_term.astype(BF16),
            key_term.astype(BF16),
            value_term.astype(BF16),
            output_term.astype(BF16),
        ),
        "dp",
    )
    part = lax.axis_index("dp")
    rows = width // lax.axis_size("dp")
    own_basis = lax.dynamic_slice_in_dim(subspace, part * rows, rows, 0)
    own_gain = lax.dynamic_slice_in_dim(gain_row, part * rows, rows, 0)[:, None]
    own_query, own_key, own_value = [
        lax.dynamic_slice_in_dim(w, part * rows, rows, 0) for w in (query_w, key_w, value_w)
    ]
    query_sum = dot("dr,re->de", own_basis, query_term)
    key_sum = dot("dr,re->de", own_basis, key_term)
    value_sum = dot("dr,re->de", own_basis, value_term)
    output_sum = dot("er,dr->ed", output_term, own_basis)
    gain_part = (
        jnp.sum(query_sum * own_query, axis=1)
        + jnp.sum(key_sum * own_key, axis=1)
        + jnp.sum(value_sum * own_value, axis=1)
    )
    grad_gain = lax.all_gather(lax.psum(gain_part, "tensor"), "dp", tiled=True)
    return (
        forward_coeffs[None],
        backward_coeffs[None],
        (query_sum * own_gain).astype(BF16)[None],
        (key_sum * own_gain).astype(BF16)[None],
        (value_sum * own_gain).astype(BF16)[None],
        output_sum.astype(BF16)[None],
        grad_gain[None],
    )


def solution(mesh):
    return jax.shard_map(
        body,
        mesh=mesh,
        in_specs=(
            P("dp", None),
            P("dp", None),
            P("pipe", "dp", None),
            P("pipe", "dp", None),
            P("pipe", "dp", None),
            P(),
            P("pipe", None),
            P("pipe", None, "tensor"),
            P("pipe", None, "tensor"),
            P("pipe", None, "tensor"),
            P("pipe", "tensor", None),
        ),
        out_specs=(
            P("pipe", "dp", None),
            P("pipe", "dp", None),
            P("pipe", "dp", "tensor"),
            P("pipe", "dp", "tensor"),
            P("pipe", "dp", "tensor"),
            P("pipe", "tensor", "dp"),
            P("pipe", None),
        ),
        check_vma=False,
    )
```

```python
import functools
import math

import jax
import jax.numpy as jnp
import numpy as np
from jax import lax
from jax.experimental import pallas as pl
from jax.experimental.pallas import tpu as pltpu
from jax.sharding import PartitionSpec as P

MESH = pl.DeviceIdType.MESH
HD = 128
HALF = HD // 2
EPSILON = 1e-05
ROPE_BASE = 500000.0
BF16 = jnp.bfloat16
F32 = jnp.float32
SCALE = 1.0 / math.sqrt(HD)
LOG2E = math.log2(math.e)
CHUNK = 512


def rope_tables(length):
    exponent = (np.float32(-2.0) * np.arange(HALF, dtype=np.float32)) / np.float32(HD)
    frequency = np.float32(ROPE_BASE) ** exponent
    angles = frequency[:, None] * np.arange(length, dtype=np.float32)[None, :]
    return np.cos(angles).astype(np.float32), np.sin(angles).astype(np.float32)


def nn(a, b):
    return jnp.dot(a, b, preferred_element_type=F32)


def nt(a, b):
    return lax.dot_general(a, b, (((1,), (1,)), ((), ())), preferred_element_type=F32)


def rope(x, cos, sin):
    x1, x2 = x[:HALF], x[HALF:]
    return jnp.concatenate([x1 * cos - x2 * sin, x2 * cos + x1 * sin], axis=0)


def undo_rope(x, cos, sin):
    x1, x2 = x[:HALF], x[HALF:]
    return jnp.concatenate([x1 * cos + x2 * sin, x2 * cos - x1 * sin], axis=0)


def main_kernel(
    sizes,
    new_coeffs,
    loss_grad,
    sent_forward,
    sent_backward,
    stashed,
    basis,
    gain,
    w_query,
    w_key,
    w_value,
    w_output,
    cos_in,
    sin_in,
    mn_out,
    fb_out,
    gg_out,
    s_v,
    st_v,
    gain_v,
    cos_v,
    sin_v,
    wq_v,
    wk_v,
    wv_v,
    wo_v,
    gw_acc,
    ws_acc,
    gram_acc,
    gw,
    gwt,
    ws,
    wst,
    gram3,
    cb,
    gb,
    cf,
    mt_acc,
    n_acc,
    dt,
    o_v,
    u_own,
    part,
    pair_send,
    pair_recv,
    rs_send,
    rs_recv,
    shard_v,
    m_v,
    n_v,
    kv_recv,
    gg_part,
    gg_recv,
    load_sem,
    in_sem,
    in_send,
    relay_send,
    pair_sem,
    rs_ssem,
    rs_rsem,
    ag_ssem,
    ag_rsem,
    own_sem,
    m_ssem,
    m_rsem,
    gg_ssem,
    gg_rsem,
):
    pipes, tensors, width, rank, heads, length = sizes
    eq = heads * HD
    p = lax.axis_index("pipe")
    z = lax.axis_index("tensor")
    n = lax.axis_index("dp")
    h = n // 2
    k = n % 2
    partner = 2 * h + 1 - k
    across = 2 * (1 - h) + k
    after = lax.rem(p + 1, pipes)
    before = lax.rem(p + pipes - 1, pipes)
    others = [(dz, dn) for dz in range(tensors) for dn in range(4) if (dz, dn) != (0, 0)]
    others = [
        (lax.rem(z + dz, tensors), lax.rem(n + dn, 4)) for dz, dn in others
    ]

    barrier = pltpu.get_barrier_semaphore()
    for oz, on in others:
        pl.semaphore_signal(barrier, inc=1, device_id=(p, oz, on), device_id_type=MESH)
    for op, on in ((before, n), (after, n), (after, across)):
        pl.semaphore_signal(barrier, inc=1, device_id=(op, z, on), device_id_type=MESH)

    steps = width // CHUNK
    col = pl.multiple_of(k * eq, HD)

    def loads(i):
        rows = pl.ds(pl.multiple_of(i * CHUNK, CHUNK), CHUNK)
        return (
            pltpu.make_async_copy(basis.at[rows, :], s_v.at[rows, :], load_sem.at[i, 0]),
            pltpu.make_async_copy(
                w_query.at[rows, pl.ds(col, eq)], wq_v.at[rows, :], load_sem.at[i, 1]
            ),
            pltpu.make_async_copy(w_key.at[rows, :], wk_v.at[rows, :], load_sem.at[i, 2]),
            pltpu.make_async_copy(w_value.at[rows, :], wv_v.at[rows, :], load_sem.at[i, 3]),
            pltpu.make_async_copy(
                w_output.at[pl.ds(col, eq), rows], wo_v.at[:, rows], load_sem.at[i, 4]
            ),
        )

    small = (
        pltpu.make_async_copy(gain, gain_v, load_sem.at[steps, 0]),
        pltpu.make_async_copy(cos_in, cos_v, load_sem.at[steps, 1]),
        pltpu.make_async_copy(sin_in, sin_v, load_sem.at[steps, 2]),
        pltpu.make_async_copy(stashed, cb.at[0], load_sem.at[steps, 3]),
    )
    small[0].start()
    for i in range(steps):
        for copy in loads(i):
            copy.start()
    for copy in small[1:]:
        copy.start()

    gw_acc[...] = jnp.zeros_like(gw_acc)
    ws_acc[...] = jnp.zeros_like(ws_acc)
    gram_acc[...] = jnp.zeros_like(gram_acc)
    small[0].wait()

    def weight_step(i, _):
        rows = pl.ds(pl.multiple_of(i * CHUNK, CHUNK), CHUNK)
        copies = loads(i)
        copies[0].wait()
        s = s_v[rows, :]
        st = s.T
        st_v[:, rows] = st
        gram_acc[...] += nn(st, s)
        stg = (st.astype(F32) * gain_v[:, rows]).astype(BF16)
        copies[1].wait()
        gw_acc[:, :eq] += nn(stg, wq_v[rows, :])
        copies[2].wait()
        gw_acc[:, eq : eq + HD] += nn(stg, wk_v[rows, :])
        copies[3].wait()
        gw_acc[:, eq + HD :] += nn(stg, wv_v[rows, :])
        copies[4].wait()
        ws_acc[...] += nn(wo_v[:, rows], s)
        return 0

    def remote(src, dst, ssem, rsem, device):
        return pltpu.make_async_remote_copy(
            src_ref=src,
            dst_ref=dst,
            send_sem=ssem,
            recv_sem=rsem,
            device_id=device,
            device_id_type=MESH,
        )

    def input_copies(grads, coeffs):
        return (
            remote(grads, gb.at[0], in_send.at[0], in_sem.at[0], (before, z, n)),
            remote(coeffs, cf.at[0], in_send.at[1], in_sem.at[1], (after, z, n)),
            remote(grads, gb.at[2], in_send.at[2], in_sem.at[2], (before, z, across)),
        )

    stash_pair = remote(stashed, cb.at[1], in_send.at[3], in_sem.at[3], (p, z, partner))
    stash_across = remote(stashed, cb.at[2], in_send.at[4], in_sem.at[4], (p, z, across))
    sends = input_copies(sent_backward, sent_forward)
    edge_sends = input_copies(loss_grad, new_coeffs)

    pl.semaphore_wait(barrier, len(others) + 3)

    @pl.when(p == 0)
    def _():
        edge_sends[0].start()

    @pl.when(p != 0)
    def _():
        sends[0].start()

    stash_pair.start()

    @pl.when(p == pipes - 1)
    def _():
        edge_sends[1].start()

    @pl.when(p != pipes - 1)
    def _():
        sends[1].start()

    @pl.when(p == 0)
    def _():
        edge_sends[2].start()

    @pl.when(p != 0)
    def _():
        sends[2].start()

    stash_across.start()

    lax.fori_loop(0, steps, weight_step, 0)

    gw_value = gw_acc[...].astype(BF16)
    gw[...] = gw_value
    gwt[...] = gw_value.T
    ws_value = ws_acc[...].astype(BF16)
    ws[...] = ws_value
    wst[...] = ws_value.T
    gram = gram_acc[...]
    first = gram.astype(BF16)
    rest = gram - first.astype(F32)
    second = rest.astype(BF16)
    gram3[0] = first
    gram3[1] = second
    gram3[2] = (rest - second.astype(F32)).astype(BF16)
    for copy in small[1:]:
        copy.wait()

    cos = cos_v[...]
    sin = sin_v[...]
    shape = (length, length)
    causal = lax.broadcasted_iota(jnp.int32, shape, 0) <= lax.broadcasted_iota(
        jnp.int32, shape, 1
    )

    def project(c):
        ct = c.T
        ut = nn(gram3[0], ct) + nn(gram3[1], ct) + nn(gram3[2], ct)
        square = jnp.sum(ut * ct.astype(F32), axis=0, keepdims=True) * (1.0 / width)
        inverse = lax.rsqrt(jnp.maximum(square, 0.0) + EPSILON)
        qkv = nn(gwt[...], ct)
        queries = [
            rope(qkv[i * HD : (i + 1) * HD] * (inverse * (SCALE * LOG2E)), cos, sin).astype(BF16)
            for i in range(heads)
        ]
        keys = rope(qkv[eq : eq + HD] * inverse, cos, sin).astype(BF16)
        values = (qkv[eq + HD :] * inverse).astype(BF16)
        return ct, ut, inverse, queries, keys, values

    def softmax(keys_rows, query):
        scores = jnp.where(causal, nn(keys_rows, query), -1e30)
        powers = jnp.exp2(scores - jnp.max(scores, axis=0, keepdims=True))
        return powers.astype(BF16), powers, 1.0 / jnp.sum(powers, axis=0, keepdims=True)

    def backward(slot, initial, own):
        c = cb[slot]
        g = gb[slot]
        ct, ut, inverse, queries, keys, values = project(c)
        keys_rows = keys.T
        values_rows = values.T
        grads = nt(ws[...], g)
        dk = jnp.zeros((HD, length), F32)
        dv = jnp.zeros((HD, length), F32)
        for i in range(heads):
            rows = slice(i * HD, (i + 1) * HD)
            low, powers, weight = softmax(keys_rows, queries[i])
            out = nn(values, low) * weight
            o_v[rows, :] = out.astype(BF16)
            grad = (grads[rows] * weight).astype(BF16)
            through = nn(values_rows, grad)
            centre = jnp.sum(grad.astype(F32) * out, axis=0, keepdims=True)
            ds = (powers * (through - centre)).astype(BF16)
            dq = undo_rope(nn(keys, ds), cos, sin)
            dt[rows, :] = (dq * (inverse * SCALE)).astype(BF16)
            dk = dk + nt(queries[i], ds)
            dv = dv + nt(grad, low)
        dt[eq : eq + HD, :] = (undo_rope(dk, cos, sin) * (inverse * (1.0 / LOG2E))).astype(BF16)
        dt[eq + HD :, :] = (dv * inverse).astype(BF16)
        d = dt[...]
        mt = nn(d, c)
        nv = nn(o_v[...], g)
        if initial:
            mt_acc[...] = mt
            n_acc[...] = nv
        else:
            mt_acc[...] += mt
            n_acc[...] += nv
        if not own:
            return None
        back = nn(gw[...], d)
        middle = jnp.sum(back * ct.astype(F32), axis=0, keepdims=True)
        return back - ut * (inverse * inverse * middle * (1.0 / width))

    def forward(slot):
        ct, ut, inverse, queries, keys, values = project(cf[slot])
        keys_rows = keys.T
        for i in range(heads):
            low, _, weight = softmax(keys_rows, queries[i])
            o_v[i * HD : (i + 1) * HD, :] = (nn(values, low) * weight).astype(BF16)
        return ut, nn(wst[...], o_v[...])

    shard = rank // tensors
    mine = pl.ds(pl.multiple_of(z * shard, shard), shard)

    def pair_copy(i):
        return remote(
            pair_send.at[i], pair_recv.at[i], pair_sem.at[i, 0], pair_sem.at[i, 1], (p, z, partner)
        )

    def scatter_copies(i):
        out = []
        for dz in range(1, tensors):
            to = lax.rem(z + dz, tensors)
            rows = pl.ds(pl.multiple_of(to * shard, shard), shard)
            out.append(
                remote(
                    rs_send.at[i, rows, :],
                    rs_recv.at[i, dz],
                    rs_ssem.at[i, dz],
                    rs_rsem.at[i, dz],
                    (p, to, n),
                )
            )
        return out

    def gather_copies(i):
        out = []
        for dz in range(1, tensors):
            to = lax.rem(z + dz, tensors)
            out.append(
                remote(
                    shard_v.at[i], fb_out.at[i, mine, :], ag_ssem.at[i, dz], ag_rsem.at[i, dz], (p, to, n)
                )
            )
        return out

    def own_copy(i):
        return pltpu.make_async_copy(shard_v.at[i], fb_out.at[i, mine, :], own_sem.at[i])

    def start_pair(i, value):
        pair_send[i] = value.astype(BF16)
        pair_copy(i).start()

    def start_scatter(i):
        pair_copy(i).wait_recv()
        total = part[i] + pair_recv[i].astype(F32)
        part[i] = total
        rs_send[i] = total.astype(BF16)
        for copy in scatter_copies(i):
            copy.start()

    def start_gather(i, extra):
        total = part[i, mine, :] + extra
        for dz, copy in enumerate(scatter_copies(i), 1):
            copy.wait_recv()
            total = total + rs_recv[i, dz].astype(F32)
        shard_v[i] = total.astype(BF16)
        for copy in gather_copies(i):
            copy.start()
        own_copy(i).start()

    relay_g0 = remote(gb.at[0], gb.at[1], relay_send.at[0], in_sem.at[5], (p, z, partner))
    relay_cf = remote(cf.at[0], cf.at[1], relay_send.at[1], in_sem.at[6], (p, z, partner))
    relay_g2 = remote(gb.at[2], gb.at[3], relay_send.at[2], in_sem.at[7], (p, z, partner))
    relay_cb = remote(cb.at[2], cb.at[3], relay_send.at[3], in_sem.at[8], (p, z, partner))

    sends[0].wait_recv()
    relay_g0.start()
    part[1] = backward(0, True, True)

    sends[1].wait_recv()
    relay_cf.start()
    stash_pair.wait_recv()
    relay_g0.wait_recv()
    start_pair(1, backward(1, False, True))

    ut, value = forward(0)
    u_own[...] = ut[...]
    part[0] = value

    sends[2].wait_recv()
    relay_g2.start()
    stash_across.wait_recv()
    relay_cb.start()
    start_scatter(1)
    relay_cf.wait_recv()
    _, value = forward(1)
    start_pair(0, value)

    own_g = gb[0]
    lift = (
        nt(gram3[0, mine, :], own_g) + nt(gram3[1, mine, :], own_g) + nt(gram3[2, mine, :], own_g)
    )
    start_gather(1, lift)
    backward(2, False, False)

    start_scatter(0)
    relay_g2.wait_recv()
    relay_cb.wait_recv()
    backward(3, False, False)

    start_gather(0, u_own[mine, :])

    m_value = mt_acc[...].astype(BF16)
    m_v[...] = m_value
    n_v[...] = n_acc[...].astype(BF16)
    kv_rows = pl.ds(2 * eq, 2 * HD)
    q_rows = pl.ds(pl.multiple_of(k * eq, eq), eq)
    n_rows = pl.ds(pl.multiple_of(2 * eq + 2 * HD + k * eq, HD), eq)
    peer = (p, z, partner)
    exchange = (
        remote(mt_acc.at[pl.ds(eq, 2 * HD), :], kv_recv, m_ssem.at[0], m_rsem.at[0], peer),
        remote(m_v.at[pl.ds(0, eq), :], mn_out.at[q_rows, :], m_ssem.at[1], m_rsem.at[1], peer),
        remote(n_v, mn_out.at[n_rows, :], m_ssem.at[2], m_rsem.at[2], peer),
    )
    keep = (
        pltpu.make_async_copy(m_v.at[pl.ds(0, eq), :], mn_out.at[q_rows, :], own_sem.at[2]),
        pltpu.make_async_copy(n_v, mn_out.at[n_rows, :], own_sem.at[3]),
    )
    for copy in exchange + keep:
        copy.start()

    m_nat = m_value.T
    half_width = width // 2
    block = half_width // 8
    for i in range(8):
        rows = pl.ds(pl.multiple_of(h * half_width + i * block, block), block)
        lifted = (
            nt(m_nat[:, :eq], wq_v[rows, :])
            + nt(m_nat[:, eq : eq + HD], wk_v[rows, :])
            + nt(m_nat[:, eq + HD :], wv_v[rows, :])
        )
        gg_part[i : i + 1, :] = jnp.sum(lifted * st_v[:, rows].astype(F32), axis=0, keepdims=True)
    me = z * 4 + n
    gg_copies = [
        remote(gg_part, gg_recv.at[me], gg_ssem.at[i], gg_rsem.at[me], (p, oz, on))
        for i, (oz, on) in enumerate(others)
    ]
    for copy in gg_copies:
        copy.start()

    exchange[0].wait_recv()
    kv_total = mt_acc[eq:, :] + kv_recv[...]
    m_v[eq:, :] = kv_total.astype(BF16)
    kv_keep = pltpu.make_async_copy(
        m_v.at[pl.ds(eq, 2 * HD), :], mn_out.at[kv_rows, :], own_sem.at[4]
    )
    kv_keep.start()

    gg_recv[me] = gg_part[...]
    for oz, on in others:
        it = oz * 4 + on
        remote(gg_part, gg_recv.at[it], gg_ssem.at[0], gg_rsem.at[it], (p, oz, on)).wait_recv()
    for hh in range(2):
        total = gg_recv[2 * hh] + gg_recv[2 * hh + 1]
        for zz in range(1, tensors):
            total = total + gg_recv[4 * zz + 2 * hh] + gg_recv[4 * zz + 2 * hh + 1]
        gg_out[8 * hh : 8 * hh + 8, :] = total

    for copy in exchange[1:]:
        copy.wait_recv()
    for copy in exchange:
        copy.wait_send()
    for copy in keep + (kv_keep,):
        copy.wait()
    for copy in gg_copies:
        copy.wait_send()
    for i in range(2):
        own_copy(i).wait()
        pair_copy(i).wait_send()
        for copy in scatter_copies(i):
            copy.wait_send()
        for copy in gather_copies(i):
            copy.wait()
    for copy in sends + (stash_pair, stash_across, relay_g0, relay_cf, relay_g2, relay_cb):
        copy.wait_send()


def slice_kernel(
    sizes,
    mn,
    fb,
    gg,
    basis,
    gain,
    forward_out,
    backward_out,
    gq_out,
    gk_out,
    gv_out,
    go_out,
    gain_out,
    mn_v,
    s_v,
    gain_v,
    gq_v,
    go_v,
    load_sem,
    out_sem,
):
    rows_own, eq, block = sizes
    n = lax.axis_index("dp")
    own = pl.ds(pl.multiple_of(n * rows_own, rows_own), rows_own)
    copies = (
        pltpu.make_async_copy(basis.at[own, :], s_v, load_sem.at[0]),
        pltpu.make_async_copy(gain.at[:, own], gain_v, load_sem.at[1]),
        pltpu.make_async_copy(mn, mn_v, load_sem.at[2]),
    )
    for copy in copies:
        copy.start()
    forward_out[...] = fb[0].T
    backward_out[...] = fb[1].T
    wide = gg.shape[1]
    for i in range(gg.shape[0]):
        gain_out[:, i * wide : (i + 1) * wide] = gg[i : i + 1, :]
    for copy in copies:
        copy.wait()
    gain_cols = jnp.broadcast_to(gain_v[...], (HD, rows_own)).T
    n_at = eq + 2 * HD

    outs = []
    for i in range(rows_own // block):
        rows = slice(i * block, (i + 1) * block)
        s = s_v[rows, :]
        scale = gain_cols[rows, :]
        for j in range(eq // HD // 2):
            cols = slice(2 * j * HD, 2 * (j + 1) * HD)
            value = nt(s, mn_v[cols, :])
            gq_v[rows, cols] = (value * jnp.concatenate([scale, scale], axis=1)).astype(BF16)
        copy = pltpu.make_async_copy(gq_v.at[rows, :], gq_out.at[rows, :], out_sem.at[i])
        copy.start()
        outs.append(copy)
        value = nt(s, mn_v[eq:n_at, :])
        gk_out[rows, :] = (value[:, :HD] * scale).astype(BF16)
        gv_out[rows, :] = (value[:, HD:] * scale).astype(BF16)
    s = s_v[...]
    for i in range(eq // block):
        rows = slice(i * block, (i + 1) * block)
        go_v[rows, :] = nt(mn_v[n_at + i * block : n_at + (i + 1) * block, :], s).astype(BF16)
        copy = pltpu.make_async_copy(
            go_v.at[rows, :], go_out.at[rows, :], out_sem.at[rows_own // block + i]
        )
        copy.start()
        outs.append(copy)
    for copy in outs:
        copy.wait()


def body(
    new_coeffs,
    loss_grad,
    sent_forward,
    sent_backward,
    stashed,
    subspace,
    norm_gain,
    w_query,
    w_key,
    w_value,
    w_output,
):
    pipes = lax.axis_size("pipe")
    tensors = lax.axis_size("tensor")
    parts = lax.axis_size("dp")
    length = new_coeffs.shape[0]
    width, rank = subspace.shape
    both = w_query.shape[2]
    eq = both // 2
    heads = eq // HD
    cos, sin = rope_tables(length)
    any_spec = pl.BlockSpec(memory_space=pl.ANY)
    vmem_spec = pl.BlockSpec(memory_space=pltpu.VMEM)
    steps = width // CHUNK
    total = 2 * both + 2 * HD
    shard = rank // tensors
    dma = pltpu.SemaphoreType.DMA
    square = (rank, rank)
    mn, fb, gg = pl.pallas_call(
        functools.partial(main_kernel, (pipes, tensors, width, rank, heads, length)),
        out_shape=(
            jax.ShapeDtypeStruct((total, rank), BF16),
            jax.ShapeDtypeStruct((2, rank, length), BF16),
            jax.ShapeDtypeStruct((16, width // 16), F32),
        ),
        in_specs=[any_spec] * 13,
        out_specs=(any_spec, any_spec, vmem_spec),
        scratch_shapes=[
            pltpu.VMEM((width, rank), BF16),
            pltpu.VMEM((rank, width), BF16),
            pltpu.VMEM((1, width), F32),
            pltpu.VMEM((HALF, length), F32),
            pltpu.VMEM((HALF, length), F32),
            pltpu.VMEM((width, eq), BF16),
            pltpu.VMEM((width, HD), BF16),
            pltpu.VMEM((width, HD), BF16),
            pltpu.VMEM((eq, width), BF16),
            pltpu.VMEM((rank, eq + 2 * HD), F32),
            pltpu.VMEM((eq, rank), F32),
            pltpu.VMEM(square, F32),
            pltpu.VMEM((rank, eq + 2 * HD), BF16),
            pltpu.VMEM((eq + 2 * HD, rank), BF16),
            pltpu.VMEM((eq, rank), BF16),
            pltpu.VMEM((rank, eq), BF16),
            pltpu.VMEM((3, rank, rank), BF16),
            pltpu.VMEM((4, length, rank), BF16),
            pltpu.VMEM((4, length, rank), BF16),
            pltpu.VMEM((2, length, rank), BF16),
            pltpu.VMEM((eq + 2 * HD, rank), F32),
            pltpu.VMEM((eq, rank), F32),
            pltpu.VMEM((eq + 2 * HD, length), BF16),
            pltpu.VMEM((eq, length), BF16),
            pltpu.VMEM((rank, length), F32),
            pltpu.VMEM((2, rank, length), F32),
            pltpu.VMEM((2, rank, length), BF16),
            pltpu.VMEM((2, rank, length), BF16),
            pltpu.VMEM((2, rank, length), BF16),
            pltpu.VMEM((2, tensors, shard, length), BF16),
            pltpu.VMEM((2, shard, length), BF16),
            pltpu.VMEM((eq + 2 * HD, rank), BF16),
            pltpu.VMEM((eq, rank), BF16),
            pltpu.VMEM((2 * HD, rank), F32),
            pltpu.VMEM((8, width // 16), F32),
            pltpu.VMEM((4 * tensors, 8, width // 16), F32),
            dma((steps + 1, 5)),
            dma((9,)),
            dma((5,)),
            dma((4,)),
            dma((2, 2)),
            dma((2, tensors)),
            dma((2, tensors)),
            dma((2, tensors)),
            dma((2, tensors)),
            dma((5,)),
            dma((3,)),
            dma((3,)),
            dma((4 * tensors,)),
            dma((4 * tensors,)),
        ],
        compiler_params=pltpu.CompilerParams(
            collective_id=0, has_side_effects=True, vmem_limit_bytes=56 * 1024 * 1024
        ),
    )(
        new_coeffs,
        loss_grad,
        sent_forward[0],
        sent_backward[0],
        stashed[0],
        subspace,
        norm_gain,
        w_query[0],
        w_key[0],
        w_value[0],
        w_output[0],
        cos,
        sin,
    )
    rows_own = width // parts
    block = 256
    outs = pl.pallas_call(
        functools.partial(slice_kernel, (rows_own, both, block)),
        out_shape=(
            jax.ShapeDtypeStruct((length, rank), BF16),
            jax.ShapeDtypeStruct((length, rank), BF16),
            jax.ShapeDtypeStruct((rows_own, both), BF16),
            jax.ShapeDtypeStruct((rows_own, HD), BF16),
            jax.ShapeDtypeStruct((rows_own, HD), BF16),
            jax.ShapeDtypeStruct((both, rows_own), BF16),
            jax.ShapeDtypeStruct((1, width), F32),
        ),
        in_specs=[any_spec, vmem_spec, vmem_spec, any_spec, any_spec],
        out_specs=(vmem_spec, vmem_spec, any_spec, vmem_spec, vmem_spec, any_spec, vmem_spec),
        scratch_shapes=[
            pltpu.VMEM((total, rank), BF16),
            pltpu.VMEM((rows_own, rank), BF16),
            pltpu.VMEM((1, rows_own), F32),
            pltpu.VMEM((rows_own, both), BF16),
            pltpu.VMEM((both, rows_own), BF16),
            dma((3,)),
            dma((rows_own // block + both // block,)),
        ],
        compiler_params=pltpu.CompilerParams(vmem_limit_bytes=56 * 1024 * 1024),
    )(mn, fb, gg, subspace, norm_gain)
    forward_out, backward_out, gq, gk, gv, go, gain_row = outs
    return (
        forward_out[None],
        backward_out[None],
        gq[None],
        gk[None],
        gv[None],
        go[None],
        gain_row,
    )


def solution(mesh):
    return jax.shard_map(
        body,
        mesh=mesh,
        in_specs=(
            P("dp", None),
            P("dp", None),
            P("pipe", "dp", None),
            P("pipe", "dp", None),
            P("pipe", "dp", None),
            P(),
            P("pipe", None),
            P("pipe", None, "tensor"),
            P("pipe", None, "tensor"),
            P("pipe", None, "tensor"),
            P("pipe", "tensor", None),
        ),
        out_specs=(
            P("pipe", "dp", None),
            P("pipe", "dp", None),
            P("pipe", "dp", "tensor"),
            P("pipe", "dp", "tensor"),
            P("pipe", "dp", "tensor"),
            P("pipe", "tensor", "dp"),
            P("pipe", None),
        ),
        check_vma=False,
    )
```

```python
import functools
import math

import jax
import jax.numpy as jnp
import numpy as np
from jax import lax
from jax.experimental import pallas as pl
from jax.experimental.pallas import tpu as pltpu
from jax.sharding import PartitionSpec as P

MESH = pl.DeviceIdType.MESH
HD = 128
HALF = HD // 2
EPSILON = 1e-05
ROPE_BASE = 500000.0
BF16 = jnp.bfloat16
F32 = jnp.float32
SCALE = 1.0 / math.sqrt(HD)
LOG2E = math.log2(math.e)
CHUNK = 512
AHEAD = 3
BEFORE = 4


def rope_tables(length):
    exponent = (np.float32(-2.0) * np.arange(HALF, dtype=np.float32)) / np.float32(HD)
    frequency = np.float32(ROPE_BASE) ** exponent
    angles = frequency[:, None] * np.arange(length, dtype=np.float32)[None, :]
    return np.cos(angles).astype(np.float32), np.sin(angles).astype(np.float32)


def nn(a, b):
    return jnp.dot(a, b, preferred_element_type=F32)


def nt(a, b):
    return lax.dot_general(a, b, (((1,), (1,)), ((), ())), preferred_element_type=F32)


def rope(x, cos, sin):
    x1, x2 = x[:HALF], x[HALF:]
    return jnp.concatenate([x1 * cos - x2 * sin, x2 * cos + x1 * sin], axis=0)


def undo_rope(x, cos, sin):
    x1, x2 = x[:HALF], x[HALF:]
    return jnp.concatenate([x1 * cos + x2 * sin, x2 * cos - x1 * sin], axis=0)


def main_kernel(
    sizes,
    new_coeffs,
    loss_grad,
    sent_forward,
    sent_backward,
    stashed,
    basis,
    gain,
    w_query,
    w_key,
    w_value,
    w_output,
    cos_in,
    sin_in,
    mn_out,
    fb_out,
    gg_out,
    s_v,
    st_v,
    gain_v,
    cos_v,
    sin_v,
    wq_v,
    wk_v,
    wv_v,
    wo_v,
    gw_acc,
    ws_acc,
    gram_acc,
    gw,
    gwt,
    ws,
    wst,
    gram3,
    cb,
    gb,
    cf,
    mt_acc,
    n_acc,
    dt,
    o_v,
    u_own,
    part,
    pair_send,
    pair_recv,
    rs_send,
    rs_recv,
    shard_v,
    m_v,
    n_v,
    kv_recv,
    gg_part,
    gg_recv,
    load_sem,
    in_sem,
    in_send,
    relay_send,
    pair_sem,
    rs_ssem,
    rs_rsem,
    ag_ssem,
    ag_rsem,
    own_sem,
    m_ssem,
    m_rsem,
    gg_ssem,
    gg_rsem,
):
    pipes, tensors, width, rank, heads, length = sizes
    eq = heads * HD
    p = lax.axis_index("pipe")
    z = lax.axis_index("tensor")
    n = lax.axis_index("dp")
    h = n // 2
    k = n % 2
    partner = 2 * h + 1 - k
    across = 2 * (1 - h) + k
    after = lax.rem(p + 1, pipes)
    before = lax.rem(p + pipes - 1, pipes)
    others = [(dz, dn) for dz in range(tensors) for dn in range(4) if (dz, dn) != (0, 0)]
    others = [
        (lax.rem(z + dz, tensors), lax.rem(n + dn, 4)) for dz, dn in others
    ]

    barrier = pltpu.get_barrier_semaphore()
    for oz, on in others:
        pl.semaphore_signal(barrier, inc=1, device_id=(p, oz, on), device_id_type=MESH)
    for op, on in ((before, n), (after, n), (after, across)):
        pl.semaphore_signal(barrier, inc=1, device_id=(op, z, on), device_id_type=MESH)

    steps = width // CHUNK
    col = pl.multiple_of(k * eq, HD)

    def loads(i):
        rows = pl.ds(pl.multiple_of(i * CHUNK, CHUNK), CHUNK)
        return (
            pltpu.make_async_copy(basis.at[rows, :], s_v.at[rows, :], load_sem.at[i, 0]),
            pltpu.make_async_copy(
                w_query.at[rows, pl.ds(col, eq)], wq_v.at[rows, :], load_sem.at[i, 1]
            ),
            pltpu.make_async_copy(w_key.at[rows, :], wk_v.at[rows, :], load_sem.at[i, 2]),
            pltpu.make_async_copy(w_value.at[rows, :], wv_v.at[rows, :], load_sem.at[i, 3]),
            pltpu.make_async_copy(
                w_output.at[pl.ds(col, eq), rows], wo_v.at[:, rows], load_sem.at[i, 4]
            ),
        )

    small = (
        pltpu.make_async_copy(gain, gain_v, load_sem.at[steps, 0]),
        pltpu.make_async_copy(cos_in, cos_v, load_sem.at[steps, 1]),
        pltpu.make_async_copy(sin_in, sin_v, load_sem.at[steps, 2]),
        pltpu.make_async_copy(stashed, cb.at[0], load_sem.at[steps, 3]),
    )
    small[0].start()
    for i in range(AHEAD):
        for copy in loads(i):
            copy.start()

    gw_acc[...] = jnp.zeros_like(gw_acc)
    ws_acc[...] = jnp.zeros_like(ws_acc)
    gram_acc[...] = jnp.zeros_like(gram_acc)
    small[0].wait()

    def weight_step(i, _):
        rows = pl.ds(pl.multiple_of(i * CHUNK, CHUNK), CHUNK)
        copies = loads(i)

        @pl.when(i + AHEAD < steps)
        def _():
            for copy in loads(i + AHEAD):
                copy.start()

        for copy in copies:
            copy.wait()
        s = s_v[rows, :]
        st = s.T
        st_v[:, rows] = st
        gram_acc[...] += nn(st, s)
        stg = (st.astype(F32) * gain_v[:, rows]).astype(BF16)
        gw_acc[:, :eq] += nn(stg, wq_v[rows, :])
        gw_acc[:, eq : eq + HD] += nn(stg, wk_v[rows, :])
        gw_acc[:, eq + HD :] += nn(stg, wv_v[rows, :])
        ws_acc[...] += nn(wo_v[:, rows], s)
        return 0

    def remote(src, dst, ssem, rsem, device):
        return pltpu.make_async_remote_copy(
            src_ref=src,
            dst_ref=dst,
            send_sem=ssem,
            recv_sem=rsem,
            device_id=device,
            device_id_type=MESH,
        )

    def input_copies(grads, coeffs):
        return (
            remote(grads, gb.at[0], in_send.at[0], in_sem.at[0], (before, z, n)),
            remote(coeffs, cf.at[0], in_send.at[1], in_sem.at[1], (after, z, n)),
            remote(grads, gb.at[2], in_send.at[2], in_sem.at[2], (before, z, across)),
        )

    stash_pair = remote(stashed, cb.at[1], in_send.at[3], in_sem.at[3], (p, z, partner))
    stash_across = remote(stashed, cb.at[2], in_send.at[4], in_sem.at[4], (p, z, across))
    sends = input_copies(sent_backward, sent_forward)
    edge_sends = input_copies(loss_grad, new_coeffs)

    lax.fori_loop(0, BEFORE, weight_step, 0)
    for copy in small[1:]:
        copy.start()
    pl.semaphore_wait(barrier, len(others) + 3)

    @pl.when(p == 0)
    def _():
        edge_sends[0].start()

    @pl.when(p != 0)
    def _():
        sends[0].start()

    stash_pair.start()

    @pl.when(p == pipes - 1)
    def _():
        edge_sends[1].start()

    @pl.when(p != pipes - 1)
    def _():
        sends[1].start()

    @pl.when(p == 0)
    def _():
        edge_sends[2].start()

    @pl.when(p != 0)
    def _():
        sends[2].start()

    stash_across.start()

    lax.fori_loop(BEFORE, steps, weight_step, 0)

    gw_value = gw_acc[...].astype(BF16)
    gw[...] = gw_value
    gwt[...] = gw_value.T
    ws_value = ws_acc[...].astype(BF16)
    ws[...] = ws_value
    wst[...] = ws_value.T
    gram = gram_acc[...]
    first = gram.astype(BF16)
    rest = gram - first.astype(F32)
    second = rest.astype(BF16)
    gram3[0] = first
    gram3[1] = second
    gram3[2] = (rest - second.astype(F32)).astype(BF16)
    for copy in small[1:]:
        copy.wait()

    cos = cos_v[...]
    sin = sin_v[...]
    shape = (length, length)
    causal = lax.broadcasted_iota(jnp.int32, shape, 0) <= lax.broadcasted_iota(
        jnp.int32, shape, 1
    )

    def project(c):
        ct = c.T
        ut = nn(gram3[0], ct) + nn(gram3[1], ct) + nn(gram3[2], ct)
        square = jnp.sum(ut * ct.astype(F32), axis=0, keepdims=True) * (1.0 / width)
        inverse = lax.rsqrt(jnp.maximum(square, 0.0) + EPSILON)
        qkv = nn(gwt[...], ct)
        queries = [
            rope(qkv[i * HD : (i + 1) * HD] * (inverse * (SCALE * LOG2E)), cos, sin).astype(BF16)
            for i in range(heads)
        ]
        keys = rope(qkv[eq : eq + HD] * inverse, cos, sin).astype(BF16)
        values = (qkv[eq + HD :] * inverse).astype(BF16)
        return ct, ut, inverse, queries, keys, values

    def softmax(pairs):
        scores = [jnp.where(causal, nn(keys_rows, query), -1e30) for keys_rows, query in pairs]
        tops = [jnp.max(x, axis=0, keepdims=True) for x in scores]
        powers = [jnp.exp2(x - top) for x, top in zip(scores, tops)]
        weights = [1.0 / jnp.sum(x, axis=0, keepdims=True) for x in powers]
        return [x.astype(BF16) for x in powers], powers, weights

    def backward(slots, initial, own):
        count = len(slots)
        many = [(j, i) for j in range(count) for i in range(heads)]
        cs = [cb[slot] for slot in slots]
        gs = [gb[slot] for slot in slots]
        projected = [project(c) for c in cs]
        cts, uts, inverses, queries, keys, values = zip(*projected)
        keys_rows = [x.T for x in keys]
        values_rows = [x.T for x in values]
        grads = [nt(ws[...], g) for g in gs]
        low, powers, weights = softmax([(keys_rows[j], queries[j][i]) for j, i in many])
        outs = [nn(values[j], x) * w for (j, _), x, w in zip(many, low, weights)]
        grad = [
            (grads[j][i * HD : (i + 1) * HD] * w).astype(BF16) for (j, i), w in zip(many, weights)
        ]
        through = [nn(values_rows[j], x) for (j, _), x in zip(many, grad)]
        centre = [jnp.sum(x.astype(F32) * y, axis=0, keepdims=True) for x, y in zip(grad, outs)]
        ds = [(x * (y - m)).astype(BF16) for x, y, m in zip(powers, through, centre)]
        dq = [nn(keys[j], x) for (j, _), x in zip(many, ds)]
        results = []
        for j in range(count):
            inverse = inverses[j]
            dk = jnp.zeros((HD, length), F32)
            dv = jnp.zeros((HD, length), F32)
            for i in range(heads):
                at = j * heads + i
                rows = slice(i * HD, (i + 1) * HD)
                o_v[j, rows, :] = outs[at].astype(BF16)
                dt[j, rows, :] = (undo_rope(dq[at], cos, sin) * (inverse * SCALE)).astype(BF16)
                dk = dk + nt(queries[j][i], ds[at])
                dv = dv + nt(grad[at], low[at])
            dt[j, eq : eq + HD, :] = (
                undo_rope(dk, cos, sin) * (inverse * (1.0 / LOG2E))
            ).astype(BF16)
            dt[j, eq + HD :, :] = (dv * inverse).astype(BF16)
            mt = nn(dt[j], cs[j])
            nv = nn(o_v[j], gs[j])
            if initial and j == 0:
                mt_acc[...] = mt
                n_acc[...] = nv
            else:
                mt_acc[...] += mt
                n_acc[...] += nv
            if own:
                back = nn(gw[...], dt[j])
                middle = jnp.sum(back * cts[j].astype(F32), axis=0, keepdims=True)
                results.append(back - uts[j] * (inverse * inverse * middle * (1.0 / width)))
        return results

    def forward(slots):
        count = len(slots)
        many = [(j, i) for j in range(count) for i in range(heads)]
        projected = [project(cf[slot]) for slot in slots]
        _, uts, _, queries, keys, values = zip(*projected)
        keys_rows = [x.T for x in keys]
        low, _, weights = softmax([(keys_rows[j], queries[j][i]) for j, i in many])
        for (j, i), x, w in zip(many, low, weights):
            o_v[j, i * HD : (i + 1) * HD, :] = (nn(values[j], x) * w).astype(BF16)
        return [(uts[j], nn(wst[...], o_v[j])) for j in range(count)]

    shard = rank // tensors
    mine = pl.ds(pl.multiple_of(z * shard, shard), shard)

    def pair_copy(i):
        return remote(
            pair_send.at[i], pair_recv.at[i], pair_sem.at[i, 0], pair_sem.at[i, 1], (p, z, partner)
        )

    def scatter_copies(i):
        out = []
        for dz in range(1, tensors):
            to = lax.rem(z + dz, tensors)
            rows = pl.ds(pl.multiple_of(to * shard, shard), shard)
            out.append(
                remote(
                    rs_send.at[i, rows, :],
                    rs_recv.at[i, dz],
                    rs_ssem.at[i, dz],
                    rs_rsem.at[i, dz],
                    (p, to, n),
                )
            )
        return out

    def gather_copies(i):
        out = []
        for dz in range(1, tensors):
            to = lax.rem(z + dz, tensors)
            out.append(
                remote(
                    shard_v.at[i], fb_out.at[i, mine, :], ag_ssem.at[i, dz], ag_rsem.at[i, dz], (p, to, n)
                )
            )
        return out

    def own_copy(i):
        return pltpu.make_async_copy(shard_v.at[i], fb_out.at[i, mine, :], own_sem.at[i])

    def start_pair(i, value):
        pair_send[i] = value.astype(BF16)
        pair_copy(i).start()

    def start_scatter(i):
        pair_copy(i).wait_recv()
        total = part[i] + pair_recv[i].astype(F32)
        part[i] = total
        rs_send[i] = total.astype(BF16)
        for copy in scatter_copies(i):
            copy.start()

    def start_gather(i, extra):
        total = part[i, mine, :] + extra
        for dz, copy in enumerate(scatter_copies(i), 1):
            copy.wait_recv()
            total = total + rs_recv[i, dz].astype(F32)
        shard_v[i] = total.astype(BF16)
        for copy in gather_copies(i):
            copy.start()
        own_copy(i).start()

    relay_g0 = remote(gb.at[0], gb.at[1], relay_send.at[0], in_sem.at[5], (p, z, partner))
    relay_cf = remote(cf.at[0], cf.at[1], relay_send.at[1], in_sem.at[6], (p, z, partner))
    relay_g2 = remote(gb.at[2], gb.at[3], relay_send.at[2], in_sem.at[7], (p, z, partner))
    relay_cb = remote(cb.at[2], cb.at[3], relay_send.at[3], in_sem.at[8], (p, z, partner))

    sends[0].wait_recv()
    relay_g0.start()
    sends[1].wait_recv()
    relay_cf.start()

    sends[2].wait_recv()
    relay_g2.start()
    stash_across.wait_recv()
    relay_cb.start()
    stash_pair.wait_recv()
    relay_g0.wait_recv()
    part[1], value = backward([0, 1], True, True)
    start_pair(1, value)

    relay_cf.wait_recv()
    (first, second) = forward([0, 1])
    u_own[...], part[0] = first
    start_pair(0, second[1])
    start_scatter(1)
    relay_g2.wait_recv()
    relay_cb.wait_recv()

    start_scatter(0)
    backward([2, 3], False, False)

    own_g = gb[0]
    lift = (
        nt(gram3[0, mine, :], own_g) + nt(gram3[1, mine, :], own_g) + nt(gram3[2, mine, :], own_g)
    )
    start_gather(1, lift)
    start_gather(0, u_own[mine, :])

    m_value = mt_acc[...].astype(BF16)
    m_v[...] = m_value
    n_v[...] = n_acc[...].astype(BF16)
    kv_rows = pl.ds(2 * eq, 2 * HD)
    q_rows = pl.ds(pl.multiple_of(k * eq, eq), eq)
    n_rows = pl.ds(pl.multiple_of(2 * eq + 2 * HD + k * eq, HD), eq)
    peer = (p, z, partner)
    exchange = (
        remote(mt_acc.at[pl.ds(eq, 2 * HD), :], kv_recv, m_ssem.at[0], m_rsem.at[0], peer),
        remote(m_v.at[pl.ds(0, eq), :], mn_out.at[q_rows, :], m_ssem.at[1], m_rsem.at[1], peer),
        remote(n_v, mn_out.at[n_rows, :], m_ssem.at[2], m_rsem.at[2], peer),
    )
    keep = (
        pltpu.make_async_copy(m_v.at[pl.ds(0, eq), :], mn_out.at[q_rows, :], own_sem.at[2]),
        pltpu.make_async_copy(n_v, mn_out.at[n_rows, :], own_sem.at[3]),
    )
    for copy in exchange + keep:
        copy.start()

    m_nat = m_value.T
    half_width = width // 2
    block = half_width // 8
    for i in range(8):
        rows = pl.ds(pl.multiple_of(h * half_width + i * block, block), block)
        lifted = (
            nt(m_nat[:, :eq], wq_v[rows, :])
            + nt(m_nat[:, eq : eq + HD], wk_v[rows, :])
            + nt(m_nat[:, eq + HD :], wv_v[rows, :])
        )
        gg_part[i : i + 1, :] = jnp.sum(lifted * st_v[:, rows].astype(F32), axis=0, keepdims=True)
    me = z * 4 + n
    gg_copies = [
        remote(gg_part, gg_recv.at[me], gg_ssem.at[i], gg_rsem.at[me], (p, oz, on))
        for i, (oz, on) in enumerate(others)
    ]
    for copy in gg_copies:
        copy.start()

    exchange[0].wait_recv()
    kv_total = mt_acc[eq:, :] + kv_recv[...]
    m_v[eq:, :] = kv_total.astype(BF16)
    kv_keep = pltpu.make_async_copy(
        m_v.at[pl.ds(eq, 2 * HD), :], mn_out.at[kv_rows, :], own_sem.at[4]
    )
    kv_keep.start()

    gg_recv[me] = gg_part[...]
    for oz, on in others:
        it = oz * 4 + on
        remote(gg_part, gg_recv.at[it], gg_ssem.at[0], gg_rsem.at[it], (p, oz, on)).wait_recv()
    for hh in range(2):
        total = gg_recv[2 * hh] + gg_recv[2 * hh + 1]
        for zz in range(1, tensors):
            total = total + gg_recv[4 * zz + 2 * hh] + gg_recv[4 * zz + 2 * hh + 1]
        for i in range(8):
            at = hh * half_width + i * block
            gg_out[:, at : at + block] = total[i : i + 1, :]

    for copy in exchange[1:]:
        copy.wait_recv()
    for copy in exchange:
        copy.wait_send()
    for copy in keep + (kv_keep,):
        copy.wait()
    for copy in gg_copies:
        copy.wait_send()
    for i in range(2):
        own_copy(i).wait()
        pair_copy(i).wait_send()
        for copy in scatter_copies(i):
            copy.wait_send()
        for copy in gather_copies(i):
            copy.wait()
    for copy in sends + (stash_pair, stash_across, relay_g0, relay_cf, relay_g2, relay_cb):
        copy.wait_send()


def slice_kernel(
    sizes,
    mn,
    fb,
    gg,
    basis,
    gain,
    forward_out,
    backward_out,
    gq_out,
    gk_out,
    gv_out,
    go_out,
    gain_out,
    mn_v,
    fb_v,
    fb_t,
    s_v,
    gain_v,
    gq_v,
    gk_v,
    gv_v,
    go_v,
    load_sem,
    out_sem,
):
    rows_own, eq, block = sizes
    n = lax.axis_index("dp")
    own = pl.ds(pl.multiple_of(n * rows_own, rows_own), rows_own)
    n_at = eq + 2 * HD
    copies = (
        pltpu.make_async_copy(basis.at[own, :], s_v, load_sem.at[0]),
        pltpu.make_async_copy(
            mn.at[pl.ds(n_at, eq), :], mn_v.at[pl.ds(n_at, eq), :], load_sem.at[1]
        ),
        pltpu.make_async_copy(gain.at[:, own], gain_v, load_sem.at[2]),
        pltpu.make_async_copy(mn.at[pl.ds(0, n_at), :], mn_v.at[pl.ds(0, n_at), :], load_sem.at[3]),
        pltpu.make_async_copy(fb, fb_v, load_sem.at[4]),
    )
    for copy in copies:
        copy.start()
    outs = []

    def send(src, dst):
        copy = pltpu.make_async_copy(src, dst, out_sem.at[len(outs)])
        copy.start()
        outs.append(copy)

    send(gg, gain_out)
    for copy in copies[:2]:
        copy.wait()
    s = s_v[...]
    for i in range(eq // block):
        rows = slice(i * block, (i + 1) * block)
        go_v[rows, :] = nt(mn_v[n_at + i * block : n_at + (i + 1) * block, :], s).astype(BF16)
        send(go_v.at[rows, :], go_out.at[rows, :])
    for copy in copies[2:]:
        copy.wait()
    gain_cols = jnp.broadcast_to(gain_v[...], (HD, rows_own)).T
    for i in range(rows_own // block):
        rows = slice(i * block, (i + 1) * block)
        s = s_v[rows, :]
        scale = gain_cols[rows, :]
        for j in range(eq // HD // 2):
            cols = slice(2 * j * HD, 2 * (j + 1) * HD)
            value = nt(s, mn_v[cols, :])
            gq_v[rows, cols] = (value * jnp.concatenate([scale, scale], axis=1)).astype(BF16)
        value = nt(s, mn_v[eq:n_at, :])
        gk_v[rows, :] = (value[:, :HD] * scale).astype(BF16)
        gv_v[rows, :] = (value[:, HD:] * scale).astype(BF16)
        send(gq_v.at[rows, :], gq_out.at[rows, :])
    send(gk_v, gk_out)
    send(gv_v, gv_out)
    fb_t[0] = fb_v[0].T
    fb_t[1] = fb_v[1].T
    send(fb_t.at[0], forward_out)
    send(fb_t.at[1], backward_out)
    for copy in outs:
        copy.wait()


def body(
    new_coeffs,
    loss_grad,
    sent_forward,
    sent_backward,
    stashed,
    subspace,
    norm_gain,
    w_query,
    w_key,
    w_value,
    w_output,
):
    pipes = lax.axis_size("pipe")
    tensors = lax.axis_size("tensor")
    parts = lax.axis_size("dp")
    length = new_coeffs.shape[0]
    width, rank = subspace.shape
    both = w_query.shape[2]
    eq = both // 2
    heads = eq // HD
    cos, sin = rope_tables(length)
    any_spec = pl.BlockSpec(memory_space=pl.ANY)
    vmem_spec = pl.BlockSpec(memory_space=pltpu.VMEM)
    steps = width // CHUNK
    total = 2 * both + 2 * HD
    shard = rank // tensors
    dma = pltpu.SemaphoreType.DMA
    square = (rank, rank)
    mn, fb, gg = pl.pallas_call(
        functools.partial(main_kernel, (pipes, tensors, width, rank, heads, length)),
        out_shape=(
            jax.ShapeDtypeStruct((total, rank), BF16),
            jax.ShapeDtypeStruct((2, rank, length), BF16),
            jax.ShapeDtypeStruct((1, width), F32),
        ),
        in_specs=[any_spec] * 13,
        out_specs=(any_spec, any_spec, vmem_spec),
        scratch_shapes=[
            pltpu.VMEM((width, rank), BF16),
            pltpu.VMEM((rank, width), BF16),
            pltpu.VMEM((1, width), F32),
            pltpu.VMEM((HALF, length), F32),
            pltpu.VMEM((HALF, length), F32),
            pltpu.VMEM((width, eq), BF16),
            pltpu.VMEM((width, HD), BF16),
            pltpu.VMEM((width, HD), BF16),
            pltpu.VMEM((eq, width), BF16),
            pltpu.VMEM((rank, eq + 2 * HD), F32),
            pltpu.VMEM((eq, rank), F32),
            pltpu.VMEM(square, F32),
            pltpu.VMEM((rank, eq + 2 * HD), BF16),
            pltpu.VMEM((eq + 2 * HD, rank), BF16),
            pltpu.VMEM((eq, rank), BF16),
            pltpu.VMEM((rank, eq), BF16),
            pltpu.VMEM((3, rank, rank), BF16),
            pltpu.VMEM((4, length, rank), BF16),
            pltpu.VMEM((4, length, rank), BF16),
            pltpu.VMEM((2, length, rank), BF16),
            pltpu.VMEM((eq + 2 * HD, rank), F32),
            pltpu.VMEM((eq, rank), F32),
            pltpu.VMEM((2, eq + 2 * HD, length), BF16),
            pltpu.VMEM((2, eq, length), BF16),
            pltpu.VMEM((rank, length), F32),
            pltpu.VMEM((2, rank, length), F32),
            pltpu.VMEM((2, rank, length), BF16),
            pltpu.VMEM((2, rank, length), BF16),
            pltpu.VMEM((2, rank, length), BF16),
            pltpu.VMEM((2, tensors, shard, length), BF16),
            pltpu.VMEM((2, shard, length), BF16),
            pltpu.VMEM((eq + 2 * HD, rank), BF16),
            pltpu.VMEM((eq, rank), BF16),
            pltpu.VMEM((2 * HD, rank), F32),
            pltpu.VMEM((8, width // 16), F32),
            pltpu.VMEM((4 * tensors, 8, width // 16), F32),
            dma((steps + 1, 5)),
            dma((9,)),
            dma((5,)),
            dma((4,)),
            dma((2, 2)),
            dma((2, tensors)),
            dma((2, tensors)),
            dma((2, tensors)),
            dma((2, tensors)),
            dma((5,)),
            dma((3,)),
            dma((3,)),
            dma((4 * tensors,)),
            dma((4 * tensors,)),
        ],
        compiler_params=pltpu.CompilerParams(
            collective_id=0, has_side_effects=True, vmem_limit_bytes=56 * 1024 * 1024
        ),
    )(
        new_coeffs,
        loss_grad,
        sent_forward[0],
        sent_backward[0],
        stashed[0],
        subspace,
        norm_gain,
        w_query[0],
        w_key[0],
        w_value[0],
        w_output[0],
        cos,
        sin,
    )
    rows_own = width // parts
    block = 256
    outs = pl.pallas_call(
        functools.partial(slice_kernel, (rows_own, both, block)),
        out_shape=(
            jax.ShapeDtypeStruct((length, rank), BF16),
            jax.ShapeDtypeStruct((length, rank), BF16),
            jax.ShapeDtypeStruct((rows_own, both), BF16),
            jax.ShapeDtypeStruct((rows_own, HD), BF16),
            jax.ShapeDtypeStruct((rows_own, HD), BF16),
            jax.ShapeDtypeStruct((both, rows_own), BF16),
            jax.ShapeDtypeStruct((1, width), F32),
        ),
        in_specs=[any_spec] * 5,
        out_specs=(any_spec,) * 7,
        scratch_shapes=[
            pltpu.VMEM((total, rank), BF16),
            pltpu.VMEM((2, rank, length), BF16),
            pltpu.VMEM((2, length, rank), BF16),
            pltpu.VMEM((rows_own, rank), BF16),
            pltpu.VMEM((1, rows_own), F32),
            pltpu.VMEM((rows_own, both), BF16),
            pltpu.VMEM((rows_own, HD), BF16),
            pltpu.VMEM((rows_own, HD), BF16),
            pltpu.VMEM((both, rows_own), BF16),
            dma((5,)),
            dma((rows_own // block + both // block + 5,)),
        ],
        compiler_params=pltpu.CompilerParams(vmem_limit_bytes=56 * 1024 * 1024),
    )(mn, fb, gg, subspace, norm_gain)
    forward_out, backward_out, gq, gk, gv, go, gain_row = outs
    return (
        forward_out[None],
        backward_out[None],
        gq[None],
        gk[None],
        gv[None],
        go[None],
        gain_row,
    )


def solution(mesh):
    return jax.shard_map(
        body,
        mesh=mesh,
        in_specs=(
            P("dp", None),
            P("dp", None),
            P("pipe", "dp", None),
            P("pipe", "dp", None),
            P("pipe", "dp", None),
            P(),
            P("pipe", None),
            P("pipe", None, "tensor"),
            P("pipe", None, "tensor"),
            P("pipe", None, "tensor"),
            P("pipe", "tensor", None),
        ),
        out_specs=(
            P("pipe", "dp", None),
            P("pipe", "dp", None),
            P("pipe", "dp", "tensor"),
            P("pipe", "dp", "tensor"),
            P("pipe", "dp", "tensor"),
            P("pipe", "tensor", "dp"),
            P("pipe", None),
        ),
        check_vma=False,
    )
```

```python
import functools
import math

import jax
import jax.numpy as jnp
import numpy as np
from jax import lax
from jax.experimental import pallas as pl
from jax.experimental.pallas import tpu as pltpu
from jax.sharding import PartitionSpec as P

MESH = pl.DeviceIdType.MESH
HD = 128
HALF = HD // 2
EPSILON = 1e-05
ROPE_BASE = 500000.0
BF16 = jnp.bfloat16
F32 = jnp.float32
SCALE = 1.0 / math.sqrt(HD)
LOG2E = math.log2(math.e)
CHUNK = 512
AHEAD = 3
BEFORE = 1
LATER = 3


def rope_tables(length):
    exponent = (np.float32(-2.0) * np.arange(HALF, dtype=np.float32)) / np.float32(HD)
    frequency = np.float32(ROPE_BASE) ** exponent
    angles = frequency[:, None] * np.arange(length, dtype=np.float32)[None, :]
    return np.cos(angles).astype(np.float32), np.sin(angles).astype(np.float32)


def nn(a, b):
    return jnp.dot(a, b, preferred_element_type=F32)


def nt(a, b):
    return lax.dot_general(a, b, (((1,), (1,)), ((), ())), preferred_element_type=F32)


def rope(x, cos, sin):
    x1, x2 = x[:HALF], x[HALF:]
    return jnp.concatenate([x1 * cos - x2 * sin, x2 * cos + x1 * sin], axis=0)


def undo_rope(x, cos, sin):
    x1, x2 = x[:HALF], x[HALF:]
    return jnp.concatenate([x1 * cos + x2 * sin, x2 * cos - x1 * sin], axis=0)


def main_kernel(
    sizes,
    new_coeffs,
    loss_grad,
    sent_forward,
    sent_backward,
    stashed,
    basis,
    gain,
    w_query,
    w_key,
    w_value,
    w_output,
    cos_in,
    sin_in,
    mn_out,
    fb_out,
    gg_out,
    s_v,
    st_v,
    gain_v,
    cos_v,
    sin_v,
    w_v,
    wo_v,
    gw_acc,
    ws_acc,
    gram_acc,
    gw,
    gwt,
    ws,
    wst,
    gram3,
    cb,
    gb,
    cf,
    mt_acc,
    n_acc,
    dt,
    o_v,
    o_f,
    u_own,
    part,
    pair_send,
    pair_recv,
    rs_send,
    rs_recv,
    shard_v,
    lift_v,
    m_v,
    n_v,
    kv_recv,
    gg_part,
    gg_pair_recv,
    gg_half,
    gg_recv,
    gg_total,
    load_sem,
    in_sem,
    in_send,
    relay_send,
    pair_sem,
    rs_ssem,
    rs_rsem,
    ag_ssem,
    ag_rsem,
    own_sem,
    m_ssem,
    m_rsem,
    gg_ssem,
    gg_rsem,
):
    pipes, tensors, width, rank, heads, length = sizes
    eq = heads * HD
    p = lax.axis_index("pipe")
    z = lax.axis_index("tensor")
    n = lax.axis_index("dp")
    h = n // 2
    k = n % 2
    partner = 2 * h + 1 - k
    across = 2 * (1 - h) + k
    after = lax.rem(p + 1, pipes)
    before = lax.rem(p + pipes - 1, pipes)
    others = [
        (lax.rem(z + dz, tensors), lax.rem(n + 2 * dh, 4))
        for dz in range(tensors)
        for dh in range(2)
        if (dz, dh) != (0, 0)
    ] + [(z, partner)]

    barrier = pltpu.get_barrier_semaphore()
    for oz, on in others:
        pl.semaphore_signal(barrier, inc=1, device_id=(p, oz, on), device_id_type=MESH)
    for op, on in ((before, n), (after, n), (after, across)):
        pl.semaphore_signal(barrier, inc=1, device_id=(op, z, on), device_id_type=MESH)

    steps = width // CHUNK
    col = pl.multiple_of(k * eq, HD)

    def loads(i):
        rows = pl.ds(pl.multiple_of(i * CHUNK, CHUNK), CHUNK)
        return (
            pltpu.make_async_copy(basis.at[rows, :], s_v.at[rows, :], load_sem.at[i, 0]),
            pltpu.make_async_copy(
                w_query.at[rows, pl.ds(col, eq)], w_v.at[rows, pl.ds(0, eq)], load_sem.at[i, 1]
            ),
            pltpu.make_async_copy(
                w_key.at[rows, :], w_v.at[rows, pl.ds(eq, HD)], load_sem.at[i, 2]
            ),
            pltpu.make_async_copy(
                w_value.at[rows, :], w_v.at[rows, pl.ds(eq + HD, HD)], load_sem.at[i, 3]
            ),
            pltpu.make_async_copy(
                w_output.at[pl.ds(col, eq), rows], wo_v.at[:, rows], load_sem.at[i, 4]
            ),
        )

    small = (
        pltpu.make_async_copy(gain, gain_v, load_sem.at[steps, 0]),
        pltpu.make_async_copy(cos_in, cos_v, load_sem.at[steps, 1]),
        pltpu.make_async_copy(sin_in, sin_v, load_sem.at[steps, 2]),
        pltpu.make_async_copy(stashed, cb.at[0], load_sem.at[steps, 3]),
    )
    small[0].start()
    for i in range(AHEAD):
        for copy in loads(i):
            copy.start()

    gw_acc[...] = jnp.zeros_like(gw_acc)
    ws_acc[...] = jnp.zeros_like(ws_acc)
    gram_acc[...] = jnp.zeros_like(gram_acc)
    small[0].wait()

    def weight_step(i, _):
        rows = pl.ds(pl.multiple_of(i * CHUNK, CHUNK), CHUNK)
        copies = loads(i)

        @pl.when(i + AHEAD < steps)
        def _():
            for copy in loads(i + AHEAD):
                copy.start()

        for copy in copies:
            copy.wait()
        s = s_v[rows, :]
        st = s.T
        st_v[:, rows] = st
        gram_acc[...] += nn(st, s)
        stg = (st.astype(F32) * gain_v[:, rows]).astype(BF16)
        gw_acc[...] += nn(stg, w_v[rows, :])
        ws_acc[...] += nn(wo_v[:, rows], s)
        return 0

    def remote(src, dst, ssem, rsem, device):
        return pltpu.make_async_remote_copy(
            src_ref=src,
            dst_ref=dst,
            send_sem=ssem,
            recv_sem=rsem,
            device_id=device,
            device_id_type=MESH,
        )

    def input_copies(grads, coeffs):
        return (
            remote(grads, gb.at[0], in_send.at[0], in_sem.at[0], (before, z, n)),
            remote(coeffs, cf.at[0], in_send.at[1], in_sem.at[1], (after, z, n)),
            remote(grads, gb.at[2], in_send.at[2], in_sem.at[2], (before, z, across)),
        )

    stash_pair = remote(stashed, cb.at[1], in_send.at[3], in_sem.at[3], (p, z, partner))
    stash_across = remote(stashed, cb.at[2], in_send.at[4], in_sem.at[4], (p, z, across))
    sends = input_copies(sent_backward, sent_forward)
    edge_sends = input_copies(loss_grad, new_coeffs)

    lax.fori_loop(0, BEFORE, weight_step, 0)
    for copy in small[1:]:
        copy.start()
    pl.semaphore_wait(barrier, len(others) + 3)

    def send_input(i, edge):
        @pl.when(p == edge)
        def _():
            edge_sends[i].start()

        @pl.when(p != edge)
        def _():
            sends[i].start()

    send_input(1, pipes - 1)
    stash_pair.start()
    lax.fori_loop(BEFORE, LATER, weight_step, 0)
    send_input(0, 0)
    send_input(2, 0)
    stash_across.start()
    lax.fori_loop(LATER, steps, weight_step, 0)

    gw_value = gw_acc[...].astype(BF16)
    gw[...] = gw_value
    gwt[...] = gw_value.T
    ws_value = ws_acc[...].astype(BF16)
    ws[...] = ws_value
    wst[...] = ws_value.T
    gram = gram_acc[...]
    first = gram.astype(BF16)
    rest = gram - first.astype(F32)
    second = rest.astype(BF16)
    gram3[0] = first
    gram3[1] = second
    gram3[2] = (rest - second.astype(F32)).astype(BF16)
    for copy in small[1:]:
        copy.wait()

    cos = cos_v[...]
    sin = sin_v[...]
    shape = (length, length)
    causal = lax.broadcasted_iota(jnp.int32, shape, 0) <= lax.broadcasted_iota(
        jnp.int32, shape, 1
    )

    def project(c):
        ct = c.T
        ut = nn(gram3[0], ct) + nn(gram3[1], ct) + nn(gram3[2], ct)
        square = jnp.sum(ut * ct.astype(F32), axis=0, keepdims=True) * (1.0 / width)
        inverse = lax.rsqrt(jnp.maximum(square, 0.0) + EPSILON)
        qkv = nn(gwt[...], ct)
        queries = [
            rope(qkv[i * HD : (i + 1) * HD] * (inverse * (SCALE * LOG2E)), cos, sin).astype(BF16)
            for i in range(heads)
        ]
        keys = rope(qkv[eq : eq + HD] * inverse, cos, sin).astype(BF16)
        values = (qkv[eq + HD :] * inverse).astype(BF16)
        return ct, ut, inverse, queries, keys, values

    def softmax(pairs):
        scores = [jnp.where(causal, nn(keys_rows, query), -1e30) for keys_rows, query in pairs]
        tops = [jnp.max(x, axis=0, keepdims=True) for x in scores]
        powers = [jnp.exp2(x - top) for x, top in zip(scores, tops)]
        weights = [1.0 / jnp.sum(x, axis=0, keepdims=True) for x in powers]
        return [x.astype(BF16) for x in powers], powers, weights

    def backward(slots, initial, own, between, later):
        count = len(slots)
        many = [(j, i) for j in range(count) for i in range(heads)]
        cs = [cb[slot] for slot in slots]
        projected = [project(c) for c in cs]
        cts, uts, inverses, queries, keys, values = zip(*projected)
        keys_rows = [x.T for x in keys]
        values_rows = [x.T for x in values]
        low, powers, weights = softmax([(keys_rows[j], queries[j][i]) for j, i in many])
        outs = [nn(values[j], x) * w for (j, _), x, w in zip(many, low, weights)]
        for at, (j, i) in enumerate(many):
            o_v[j, i * HD : (i + 1) * HD, :] = outs[at].astype(BF16)
        between()
        gs = [gb[slot] for slot in slots]
        grads = [nt(ws[...], g) for g in gs]
        grad = [
            (grads[j][i * HD : (i + 1) * HD] * w).astype(BF16) for (j, i), w in zip(many, weights)
        ]
        through = [nn(values_rows[j], x) for (j, _), x in zip(many, grad)]
        centre = [jnp.sum(x.astype(F32) * y, axis=0, keepdims=True) for x, y in zip(grad, outs)]
        ds = [(x * (y - m)).astype(BF16) for x, y, m in zip(powers, through, centre)]
        dq = [nn(keys[j], x) for (j, _), x in zip(many, ds)]
        for at, (j, i) in enumerate(many):
            value = undo_rope(dq[at], cos, sin) * (inverses[j] * SCALE)
            dt[j, i * HD : (i + 1) * HD, :] = value.astype(BF16)
        for j in range(count):
            nv = nn(o_v[j], gs[j])
            if initial and j == 0:
                n_acc[...] = nv
            else:
                n_acc[...] += nv
        later()
        results = []
        for j in range(count):
            inverse = inverses[j]
            dk = jnp.zeros((HD, length), F32)
            dv = jnp.zeros((HD, length), F32)
            for i in range(heads):
                at = j * heads + i
                dk = dk + nt(queries[j][i], ds[at])
                dv = dv + nt(grad[at], low[at])
            dt[j, eq : eq + HD, :] = (
                undo_rope(dk, cos, sin) * (inverse * (1.0 / LOG2E))
            ).astype(BF16)
            dt[j, eq + HD :, :] = (dv * inverse).astype(BF16)
            mt = nn(dt[j], cs[j])
            if initial and j == 0:
                mt_acc[...] = mt
            else:
                mt_acc[...] += mt
            if own:
                back = nn(gw[...], dt[j])
                middle = jnp.sum(back * cts[j].astype(F32), axis=0, keepdims=True)
                results.append(back - uts[j] * (inverse * inverse * middle * (1.0 / width)))
        return results

    def forward(slots):
        count = len(slots)
        many = [(j, i) for j in range(count) for i in range(heads)]
        projected = [project(cf[slot]) for slot in slots]
        _, uts, _, queries, keys, values = zip(*projected)
        keys_rows = [x.T for x in keys]
        low, _, weights = softmax([(keys_rows[j], queries[j][i]) for j, i in many])
        for (j, i), x, w in zip(many, low, weights):
            o_f[j, i * HD : (i + 1) * HD, :] = (nn(values[j], x) * w).astype(BF16)
        return [(uts[j], nn(wst[...], o_f[j])) for j in range(count)]

    shard = rank // tensors
    mine = pl.ds(pl.multiple_of(z * shard, shard), shard)

    def pair_copy(i):
        return remote(
            pair_send.at[i], pair_recv.at[i], pair_sem.at[i, 0], pair_sem.at[i, 1], (p, z, partner)
        )

    def scatter_copies(i):
        out = []
        for dz in range(1, tensors):
            to = lax.rem(z + dz, tensors)
            rows = pl.ds(pl.multiple_of(to * shard, shard), shard)
            out.append(
                remote(
                    rs_send.at[i, rows, :],
                    rs_recv.at[i, dz],
                    rs_ssem.at[i, dz],
                    rs_rsem.at[i, dz],
                    (p, to, n),
                )
            )
        return out

    def gather_copies(i):
        out = []
        for dz in range(1, tensors):
            to = lax.rem(z + dz, tensors)
            out.append(
                remote(
                    shard_v.at[i], fb_out.at[i, mine, :], ag_ssem.at[i, dz], ag_rsem.at[i, dz], (p, to, n)
                )
            )
        return out

    def own_copy(i):
        return pltpu.make_async_copy(shard_v.at[i], fb_out.at[i, mine, :], own_sem.at[i])

    def start_pair(i, value):
        pair_send[i] = value.astype(BF16)
        pair_copy(i).start()

    def start_scatter(i):
        pair_copy(i).wait_recv()
        total = part[i] + pair_recv[i].astype(F32)
        part[i] = total
        rs_send[i] = total.astype(BF16)
        for copy in scatter_copies(i):
            copy.start()

    def start_gather(i, extra):
        total = part[i, mine, :] + extra
        for dz, copy in enumerate(scatter_copies(i), 1):
            copy.wait_recv()
            total = total + rs_recv[i, dz].astype(F32)
        shard_v[i] = total.astype(BF16)
        for copy in gather_copies(i):
            copy.start()
        own_copy(i).start()

    relay_g0 = remote(gb.at[0], gb.at[1], relay_send.at[0], in_sem.at[5], (p, z, partner))
    relay_cf = remote(cf.at[0], cf.at[1], relay_send.at[1], in_sem.at[6], (p, z, partner))
    relay_g2 = remote(gb.at[2], gb.at[3], relay_send.at[2], in_sem.at[7], (p, z, partner))
    relay_cb = remote(cb.at[2], cb.at[3], relay_send.at[3], in_sem.at[8], (p, z, partner))

    q_rows = pl.ds(pl.multiple_of(k * eq, eq), eq)
    kv_rows = pl.ds(2 * eq, 2 * HD)
    n_rows = pl.ds(pl.multiple_of(2 * eq + 2 * HD + k * eq, HD), eq)
    own_m = m_v.at[pl.ds(0, eq), :]
    own_kv = m_v.at[pl.ds(eq, 2 * HD), :]
    peer = (p, z, partner)
    exchange = (
        remote(n_v, mn_out.at[n_rows, :], m_ssem.at[0], m_rsem.at[0], peer),
        remote(mt_acc.at[pl.ds(eq, 2 * HD), :], kv_recv, m_ssem.at[1], m_rsem.at[1], peer),
        remote(own_m, mn_out.at[q_rows, :], m_ssem.at[2], m_rsem.at[2], peer),
    )
    keep = (
        pltpu.make_async_copy(n_v, mn_out.at[n_rows, :], own_sem.at[2]),
        pltpu.make_async_copy(own_m, mn_out.at[q_rows, :], own_sem.at[3]),
        pltpu.make_async_copy(own_kv, mn_out.at[kv_rows, :], own_sem.at[4]),
    )

    chips = [(dz, dh) for dz in range(tensors) for dh in range(2) if (dz, dh) != (0, 0)]
    gg_pair = remote(
        gg_part.at[1 - k], gg_pair_recv, gg_ssem.at[0], gg_rsem.at[0], (p, z, partner)
    )
    gg_last = remote(gg_total.at[k], gg_total.at[k], gg_ssem.at[1], gg_rsem.at[1], (p, z, partner))
    gg_copies = [
        remote(
            gg_half,
            gg_recv.at[i],
            gg_ssem.at[i + 2],
            gg_rsem.at[i + 2],
            (p, lax.rem(z + dz, tensors), lax.rem(n + 2 * dh, 4)),
        )
        for i, (dz, dh) in enumerate(chips)
    ]

    def gain_stage():
        gg_pair.wait_recv()
        gg_half[...] = gg_part[k] + gg_pair_recv[...]
        for copy in gg_copies:
            copy.start()

    def gain_finish():
        total = gg_half[...]
        for copy in gg_copies:
            copy.wait_recv()
        for i in range(len(gg_copies)):
            total = total + gg_recv[i]
        gg_total[k] = total
        gg_last.start()

    block = width // 8
    fine = width // 16

    def gain_terms():
        terms = mt_acc[...].astype(BF16)
        for i in range(8):
            rows = slice(i * block, (i + 1) * block)
            lifted = nn(w_v[rows, :], terms)
            product = lifted * s_v[rows, :].astype(F32)
            product = sum(product[:, j : j + HD] for j in range(HD, rank, HD)) + product[:, :HD]
            row = jnp.sum(product.T, axis=0, keepdims=True)
            at = 2 * (i % 4)
            gg_part[i // 4, at : at + 1, :] = row[:, :fine]
            gg_part[i // 4, at + 1 : at + 2, :] = row[:, fine:]
        gg_pair.start()

    def between_own():
        sends[0].wait_recv()
        relay_g0.start()
        relay_cf.wait_recv()
        first, second = forward([0, 1])
        u_own[...], part[0] = first
        start_pair(0, second[1])
        relay_g0.wait_recv()

    def between_across():
        relay_g2.wait_recv()
        gain_stage()
        own_g = gb[0]
        lift_v[...] = (
            nt(gram3[0, mine, :], own_g)
            + nt(gram3[1, mine, :], own_g)
            + nt(gram3[2, mine, :], own_g)
        )

    def later_across():
        n_v[...] = n_acc[...].astype(BF16)
        exchange[0].start()
        keep[0].start()
        start_gather(0, u_own[mine, :])

    sends[1].wait_recv()
    relay_cf.start()
    stash_pair.wait_recv()
    part[1], value = backward([0, 1], True, True, between_own, lambda: None)
    start_pair(1, value)
    start_scatter(0)
    sends[2].wait_recv()
    relay_g2.start()
    stash_across.wait_recv()
    relay_cb.start()
    gain_terms()
    start_scatter(1)
    relay_cb.wait_recv()
    backward([2, 3], False, False, between_across, later_across)

    exchange[1].start()
    m_v[:eq, :] = mt_acc[:eq, :].astype(BF16)
    exchange[2].start()
    keep[1].start()
    start_gather(1, lift_v[...])
    gain_finish()
    exchange[1].wait_recv()
    m_v[eq:, :] = (mt_acc[eq:, :] + kv_recv[...]).astype(BF16)
    keep[2].start()
    gg_last.wait_recv()
    for i in range(2):
        for j in range(8):
            at = (i * 8 + j) * fine
            gg_out[:, at : at + fine] = gg_total[i, j : j + 1, :]

    exchange[0].wait_recv()
    exchange[2].wait_recv()
    for copy in exchange:
        copy.wait_send()
    for copy in keep:
        copy.wait()
    for copy in gg_copies + [gg_pair, gg_last]:
        copy.wait_send()
    for i in range(2):
        own_copy(i).wait()
        pair_copy(i).wait_send()
        for copy in scatter_copies(i):
            copy.wait_send()
        for copy in gather_copies(i):
            copy.wait()
    for copy in sends + (stash_pair, stash_across, relay_g0, relay_cf, relay_g2, relay_cb):
        copy.wait_send()


def slice_kernel(
    sizes,
    mn,
    fb,
    gg,
    basis,
    gain,
    forward_out,
    backward_out,
    gq_out,
    gk_out,
    gv_out,
    go_out,
    gain_out,
    mn_v,
    fb_v,
    fb_t,
    s_v,
    gain_v,
    gq_v,
    gk_v,
    gv_v,
    go_v,
    load_sem,
    out_sem,
):
    rows_own, eq, block = sizes
    n = lax.axis_index("dp")
    own = pl.ds(pl.multiple_of(n * rows_own, rows_own), rows_own)
    n_at = eq + 2 * HD
    copies = (
        pltpu.make_async_copy(basis.at[own, :], s_v, load_sem.at[0]),
        pltpu.make_async_copy(
            mn.at[pl.ds(n_at, eq), :], mn_v.at[pl.ds(n_at, eq), :], load_sem.at[1]
        ),
        pltpu.make_async_copy(gain.at[:, own], gain_v, load_sem.at[2]),
        pltpu.make_async_copy(mn.at[pl.ds(0, n_at), :], mn_v.at[pl.ds(0, n_at), :], load_sem.at[3]),
        pltpu.make_async_copy(fb, fb_v, load_sem.at[4]),
    )
    for copy in copies:
        copy.start()
    outs = []

    def send(src, dst):
        copy = pltpu.make_async_copy(src, dst, out_sem.at[len(outs)])
        copy.start()
        outs.append(copy)

    send(gg, gain_out)
    for copy in copies[:2]:
        copy.wait()
    s = s_v[...]
    for i in range(eq // block):
        rows = slice(i * block, (i + 1) * block)
        go_v[rows, :] = nt(mn_v[n_at + i * block : n_at + (i + 1) * block, :], s).astype(BF16)
        send(go_v.at[rows, :], go_out.at[rows, :])
    for copy in copies[2:]:
        copy.wait()
    gain_cols = jnp.broadcast_to(gain_v[...], (HD, rows_own)).T
    for i in range(rows_own // block):
        rows = slice(i * block, (i + 1) * block)
        s = s_v[rows, :]
        scale = gain_cols[rows, :]
        for j in range(eq // HD // 2):
            cols = slice(2 * j * HD, 2 * (j + 1) * HD)
            value = nt(s, mn_v[cols, :])
            gq_v[rows, cols] = (value * jnp.concatenate([scale, scale], axis=1)).astype(BF16)
        value = nt(s, mn_v[eq:n_at, :])
        gk_v[rows, :] = (value[:, :HD] * scale).astype(BF16)
        gv_v[rows, :] = (value[:, HD:] * scale).astype(BF16)
        send(gq_v.at[rows, :], gq_out.at[rows, :])
    send(gk_v, gk_out)
    send(gv_v, gv_out)
    fb_t[0] = fb_v[0].T
    fb_t[1] = fb_v[1].T
    send(fb_t.at[0], forward_out)
    send(fb_t.at[1], backward_out)
    for copy in outs:
        copy.wait()


def body(
    new_coeffs,
    loss_grad,
    sent_forward,
    sent_backward,
    stashed,
    subspace,
    norm_gain,
    w_query,
    w_key,
    w_value,
    w_output,
):
    pipes = lax.axis_size("pipe")
    tensors = lax.axis_size("tensor")
    parts = lax.axis_size("dp")
    length = new_coeffs.shape[0]
    width, rank = subspace.shape
    both = w_query.shape[2]
    eq = both // 2
    heads = eq // HD
    cos, sin = rope_tables(length)
    any_spec = pl.BlockSpec(memory_space=pl.ANY)
    vmem_spec = pl.BlockSpec(memory_space=pltpu.VMEM)
    steps = width // CHUNK
    total = 2 * both + 2 * HD
    shard = rank // tensors
    dma = pltpu.SemaphoreType.DMA
    square = (rank, rank)
    mn, fb, gg = pl.pallas_call(
        functools.partial(main_kernel, (pipes, tensors, width, rank, heads, length)),
        out_shape=(
            jax.ShapeDtypeStruct((total, rank), BF16),
            jax.ShapeDtypeStruct((2, rank, length), BF16),
            jax.ShapeDtypeStruct((1, width), F32),
        ),
        in_specs=[any_spec] * 13,
        out_specs=(any_spec, any_spec, vmem_spec),
        scratch_shapes=[
            pltpu.VMEM((width, rank), BF16),
            pltpu.VMEM((rank, width), BF16),
            pltpu.VMEM((1, width), F32),
            pltpu.VMEM((HALF, length), F32),
            pltpu.VMEM((HALF, length), F32),
            pltpu.VMEM((width, eq + 2 * HD), BF16),
            pltpu.VMEM((eq, width), BF16),
            pltpu.VMEM((rank, eq + 2 * HD), F32),
            pltpu.VMEM((eq, rank), F32),
            pltpu.VMEM(square, F32),
            pltpu.VMEM((rank, eq + 2 * HD), BF16),
            pltpu.VMEM((eq + 2 * HD, rank), BF16),
            pltpu.VMEM((eq, rank), BF16),
            pltpu.VMEM((rank, eq), BF16),
            pltpu.VMEM((3, rank, rank), BF16),
            pltpu.VMEM((4, length, rank), BF16),
            pltpu.VMEM((4, length, rank), BF16),
            pltpu.VMEM((2, length, rank), BF16),
            pltpu.VMEM((eq + 2 * HD, rank), F32),
            pltpu.VMEM((eq, rank), F32),
            pltpu.VMEM((2, eq + 2 * HD, length), BF16),
            pltpu.VMEM((2, eq, length), BF16),
            pltpu.VMEM((2, eq, length), BF16),
            pltpu.VMEM((rank, length), F32),
            pltpu.VMEM((2, rank, length), F32),
            pltpu.VMEM((2, rank, length), BF16),
            pltpu.VMEM((2, rank, length), BF16),
            pltpu.VMEM((2, rank, length), BF16),
            pltpu.VMEM((2, tensors, shard, length), BF16),
            pltpu.VMEM((2, shard, length), BF16),
            pltpu.VMEM((shard, length), F32),
            pltpu.VMEM((eq + 2 * HD, rank), BF16),
            pltpu.VMEM((eq, rank), BF16),
            pltpu.VMEM((2 * HD, rank), F32),
            pltpu.VMEM((2, 8, width // 16), F32),
            pltpu.VMEM((8, width // 16), F32),
            pltpu.VMEM((8, width // 16), F32),
            pltpu.VMEM((2 * tensors, 8, width // 16), F32),
            pltpu.VMEM((2, 8, width // 16), F32),
            dma((steps + 1, 5)),
            dma((9,)),
            dma((5,)),
            dma((4,)),
            dma((2, 2)),
            dma((2, tensors)),
            dma((2, tensors)),
            dma((2, tensors)),
            dma((2, tensors)),
            dma((5,)),
            dma((3,)),
            dma((3,)),
            dma((2 * tensors + 1,)),
            dma((2 * tensors + 1,)),
        ],
        compiler_params=pltpu.CompilerParams(
            collective_id=0, has_side_effects=True, vmem_limit_bytes=56 * 1024 * 1024
        ),
    )(
        new_coeffs,
        loss_grad,
        sent_forward[0],
        sent_backward[0],
        stashed[0],
        subspace,
        norm_gain,
        w_query[0],
        w_key[0],
        w_value[0],
        w_output[0],
        cos,
        sin,
    )
    rows_own = width // parts
    block = 256
    outs = pl.pallas_call(
        functools.partial(slice_kernel, (rows_own, both, block)),
        out_shape=(
            jax.ShapeDtypeStruct((length, rank), BF16),
            jax.ShapeDtypeStruct((length, rank), BF16),
            jax.ShapeDtypeStruct((rows_own, both), BF16),
            jax.ShapeDtypeStruct((rows_own, HD), BF16),
            jax.ShapeDtypeStruct((rows_own, HD), BF16),
            jax.ShapeDtypeStruct((both, rows_own), BF16),
            jax.ShapeDtypeStruct((1, width), F32),
        ),
        in_specs=[any_spec] * 5,
        out_specs=(any_spec,) * 7,
        scratch_shapes=[
            pltpu.VMEM((total, rank), BF16),
            pltpu.VMEM((2, rank, length), BF16),
            pltpu.VMEM((2, length, rank), BF16),
            pltpu.VMEM((rows_own, rank), BF16),
            pltpu.VMEM((1, rows_own), F32),
            pltpu.VMEM((rows_own, both), BF16),
            pltpu.VMEM((rows_own, HD), BF16),
            pltpu.VMEM((rows_own, HD), BF16),
            pltpu.VMEM((both, rows_own), BF16),
            dma((5,)),
            dma((rows_own // block + both // block + 5,)),
        ],
        compiler_params=pltpu.CompilerParams(vmem_limit_bytes=56 * 1024 * 1024),
    )(mn, fb, gg, subspace, norm_gain)
    forward_out, backward_out, gq, gk, gv, go, gain_row = outs
    return (
        forward_out[None],
        backward_out[None],
        gq[None],
        gk[None],
        gv[None],
        go[None],
        gain_row,
    )


def solution(mesh):
    return jax.shard_map(
        body,
        mesh=mesh,
        in_specs=(
            P("dp", None),
            P("dp", None),
            P("pipe", "dp", None),
            P("pipe", "dp", None),
            P("pipe", "dp", None),
            P(),
            P("pipe", None),
            P("pipe", None, "tensor"),
            P("pipe", None, "tensor"),
            P("pipe", None, "tensor"),
            P("pipe", "tensor", None),
        ),
        out_specs=(
            P("pipe", "dp", None),
            P("pipe", "dp", None),
            P("pipe", "dp", "tensor"),
            P("pipe", "dp", "tensor"),
            P("pipe", "dp", "tensor"),
            P("pipe", "tensor", "dp"),
            P("pipe", None),
        ),
        check_vma=False,
    )
```
